512 devices in a mesh: dp: 32 (over y, x), pipe: 16 (over z, core).
Axes of the slice: x: 4, y: 8, z: 8, core: 2. Of those that a mesh axis runs over, the one named last changes fastest.
Arguments:
- base_ids: int32 [32, 3, 64, 32], P('dp'), may hold values from 0 to 3
- embed_table: bfloat16 [128, 768], replicated, may hold values from -1 to 1
- segment_weights: bfloat16 [16, 768, 768], P('pipe'), may hold values from -0.21875 to 0.21875
- conv_taps: float32 [16, 3, 768], P('pipe'), may hold values from -3 to 3
- norm_gains: float32 [16, 768], P('pipe'), may hold values from 0.1 to 1.9
- cotangent: bfloat16 [32, 3, 64, 768], P('dp'), may hold values from -6 to 6
Outputs:
- weight_grads: float32 [16, 768, 768], P('pipe')
The draws below stay inside these ranges and needn't reach their ends.
All inputs are finite; a program needn't handle non-finite values.
Results may differ from the reference program's by a relative error of at most 0.023.
Values may be sent and summed in bfloat16 or wider, within the bound.
No kernel may reach another device: no remote copies, remote signals or barrier semaphores. Data moves between devices by JAX's collectives and lax.ppermute only.
A program may use at most 64 MiB of HBM per device.

```python
import math
import jax
import jax.numpy as jnp
from jax import lax

C = 768
BIN = 32
ROWS = 64
MICRO = 3
WINDOWS = 32
SEGMENTS = 16
N_DP = 32
N_PIPE = 16


def with_ends(array, own_key, low, top_value):
    longest = array.shape.index(max(array.shape))
    spots = []
    for shift in (0, 1):
        where = [jax.random.randint(jax.random.fold_in(own_key, axis), (), 0, length) for axis, length in enumerate(array.shape)]
        where[longest] = (where[longest] + shift) % array.shape[longest]
        spots.append(tuple(where))
    return array.at[spots[0]].set(low).at[spots[1]].set(top_value)


def block_scale(stream_key, shape, pieces, low, largest):
    gain = 1.0
    for dim, shards_of in pieces:
        draws = jax.random.uniform(jax.random.fold_in(jax.random.fold_in(stream_key, 6), dim), (shards_of,), jnp.float32, low / len(pieces), largest / len(pieces))
        gain = gain * jnp.repeat(jnp.exp(draws), shape[dim] // shards_of).reshape((-1,) + (1,) * (len(shape) - 1 - dim))
    return gain


def normal_values(key, extent, deviation, most, split=(), kind=jnp.bfloat16):
    drawn = deviation * jax.random.normal(key, extent, jnp.float32)
    if split:
        drawn = drawn * block_scale(key, extent, split, -0.22, 0.18)
    return jnp.clip(drawn, -most, most).astype(kind)


def setup_inputs(seed: int = 0) -> dict:
    seeds = jax.random.split(jax.random.key(seed), 7)
    base_ids = with_ends(jax.random.randint(seeds[0], (WINDOWS, MICRO, ROWS, BIN), 0, 4), jax.random.fold_in(seeds[0], 1), 0, 3).astype(jnp.int32)
    embed_table = normal_values(seeds[1], (4 * BIN, C), BIN ** -0.5, 1.0)
    segment_weights = normal_values(seeds[2], (SEGMENTS, C, C), C ** -0.5, 0.21875, ((0, 16),))
    conv_taps = normal_values(seeds[3], (SEGMENTS, 3, C), 0.6, 3.0, ((0, 16),), jnp.float32)
    norm_gains = jnp.clip(1.0 + 0.18 * jax.random.normal(seeds[4], (SEGMENTS, C), jnp.float32), 0.1, 1.9)
    cotangent = normal_values(seeds[5], (WINDOWS, MICRO, ROWS, C), 1.0, 6.0, ((0, 32),))
    return {"base_ids": base_ids, "embed_table": embed_table, "segment_weights": segment_weights, "conv_taps": conv_taps, "norm_gains": norm_gains, "cotangent": cotangent}


def encode_bases(base_rows, embed_table):
    one_hot = (base_rows[:, :, None] == jnp.arange(4, dtype=jnp.int32)).astype(jnp.bfloat16)
    one_hot = one_hot.reshape(base_rows.shape[0], -1)
    return jnp.dot(one_hot, embed_table, preferred_element_type=jnp.float32).astype(jnp.bfloat16)

def section_parts(segment_input, skip_input, tap_rows, gain_row):
    inner_sum = segment_input.astype(jnp.float32) + skip_input.astype(jnp.float32)
    inv_rms = lax.rsqrt(lax.optimization_barrier(jnp.mean(inner_sum * inner_sum, axis=-1, keepdims=True)) + 1e-06)
    normed = inner_sum * inv_rms * gain_row
    padded = jnp.pad(normed, ((1, 1), (0, 0)))
    mixed = tap_rows[0] * padded[:-2] + tap_rows[1] * padded[1:-1] + tap_rows[2] * padded[2:]
    return (inner_sum, jax.nn.gelu(mixed))

def section_forward(segment_input, skip_input, weight, tap_rows, gain_row):
    inner_sum, act_full = section_parts(segment_input, skip_input, tap_rows, gain_row)
    product = jnp.dot(act_full.astype(jnp.bfloat16), weight, preferred_element_type=jnp.float32)
    return (inner_sum + product).astype(jnp.bfloat16)

def section_back(segment_input, skip_input, weight, tap_rows, gain_row, upstream):
    upstream_bf = upstream.astype(jnp.bfloat16)
    primal, pullback = jax.vjp(lambda first_in, second_in: section_parts(first_in, second_in, tap_rows, gain_row), segment_input, skip_input)
    act_bf = primal[1].astype(jnp.bfloat16)
    weight_term = lax.dot_general(act_bf, upstream_bf, (((0,), (0,)), ((), ())), preferred_element_type=jnp.float32)
    act_grad = lax.dot_general(upstream_bf, weight, (((1,), (1,)), ((), ())), preferred_element_type=jnp.float32)
    input_grad, skip_grad = pullback((upstream, act_grad))
    return (input_grad, skip_grad, weight_term)

def reference(base_ids, embed_table, segment_weights, conv_taps, norm_gains, cotangent):
    quarter = N_PIPE // 4
    zero_rows = jnp.zeros((ROWS, C), jnp.bfloat16)

    def window(total, inputs):
        window_bases, window_cot = inputs
        for micro_index in range(MICRO):
            segment_input = encode_bases(window_bases[micro_index], embed_table)
            stored_inputs = []
            stored_skips = []
            towers = []
            for segment in range(N_PIPE):
                skip_input = towers[segment - 3 * quarter] if segment >= 3 * quarter else zero_rows
                stored_inputs.append(segment_input)
                stored_skips.append(skip_input)
                output = section_forward(segment_input, skip_input, segment_weights[segment], conv_taps[segment], norm_gains[segment])
                if segment < quarter:
                    towers.append(output)
                segment_input = output
            returned = [zero_rows for _ in range(quarter)]
            upstream = window_cot[micro_index].astype(jnp.float32)
            for segment in reversed(range(N_PIPE)):
                if segment < quarter:
                    upstream = upstream + returned[segment].astype(jnp.float32)
                input_grad, skip_grad, weight_term = section_back(stored_inputs[segment], stored_skips[segment], segment_weights[segment], conv_taps[segment], norm_gains[segment], upstream)
                total = total.at[segment].add(weight_term)
                if segment >= 3 * quarter:
                    returned[segment - 3 * quarter] = skip_grad
                upstream = input_grad.astype(jnp.float32)
        return (total, None)
    total, _ = lax.scan(window, jnp.zeros((N_PIPE, C, C), jnp.float32), (base_ids, cotangent))
    return total * (1.0 / math.sqrt(N_DP * MICRO * ROWS))
```

```python
import functools
import math

import jax
import jax.numpy as jnp
from jax import lax
from jax.experimental import pallas as pl
from jax.experimental.pallas import tpu as pltpu
from jax.sharding import PartitionSpec as P

GROUP = 4
MICROS = 3
CHUNK = 256
ANY = pl.BlockSpec(memory_space=pl.ANY)
VM = pl.BlockSpec(memory_space=pltpu.VMEM)
SM = pl.BlockSpec(memory_space=pltpu.SMEM)
PARAMS = pltpu.CompilerParams(vmem_limit_bytes=40 * 1024 * 1024)
CUBIC = 0.044715
SCALE = math.sqrt(2.0 / math.pi)


def row_before(block):
    rows = lax.broadcasted_iota(jnp.int32, block.shape, 0)
    return jnp.where(rows == 0, 0.0, pltpu.roll(block, 1, 0))


def row_after(block):
    size = block.shape[0]
    rows = lax.broadcasted_iota(jnp.int32, block.shape, 0)
    return jnp.where(rows == size - 1, 0.0, pltpu.roll(block, size - 1, 0))


def chunks_of(channels):
    return [slice(c, c + CHUNK) for c in range(0, channels, CHUNK)]


def start_weights(member, order, sources, wbuf, wsem):
    for j in order:
        for d in range(GROUP):

            @pl.when(jnp.bitwise_xor(member, j) == d)
            def _():
                pltpu.make_async_copy(sources[d], wbuf.at[d], wsem.at[d]).start()


def forward_kernel(stage, skip, towers, flags, x_ref, w0, w1, w2, w3, par_ref, *rest):
    rest = list(rest)
    k_ref = rest.pop(0) if skip else None
    rest.pop(0)
    y_ref, uh_hbm, gp_hbm, inv_hbm, h_hbm = rest[:5]
    rest = rest[5:]
    ys_hbm = rest.pop(0) if towers else None
    wbuf, ub, uh, gp, inv_b, hb, yb, wsem, osem = rest
    channels = x_ref.shape[1]
    member = flags[1]

    @pl.when((flags[0] == stage) & (member < MICROS))
    def _():
        start_weights(member, range(GROUP), (w0, w1, w2, w3), wbuf, wsem)
        copies = []
        for j in range(GROUP):
            d = jnp.bitwise_xor(member, j)
            squares = None
            for cs in chunks_of(channels):
                if j == 0:
                    u = x_ref[:, cs].astype(jnp.float32)
                else:
                    u = yb[j - 1, :, cs].astype(jnp.float32)
                if skip:
                    u = u + k_ref[j, :, cs].astype(jnp.float32)
                ub[:, cs] = u
                part = jnp.sum(u * u, axis=-1, keepdims=True)
                squares = part if squares is None else squares + part
            inv = lax.rsqrt(squares * (1.0 / channels) + 1e-06)
            inv_b[j] = jnp.broadcast_to(inv, inv_b.shape[1:])
            pltpu.make_async_copy(w0, wbuf.at[d], wsem.at[d]).wait()
            total = None
            for cs in chunks_of(channels):
                unit = ub[:, cs] * inv
                uh[j, :, cs] = unit
                n = unit * par_ref[d, 3:4, cs]
                v = (
                    par_ref[d, 0:1, cs] * row_before(n)
                    + par_ref[d, 1:2, cs] * n
                    + par_ref[d, 2:3, cs] * row_after(n)
                )
                v2 = v * v
                th = jnp.tanh(v * (SCALE + (SCALE * CUBIC) * v2))
                half = 0.5 * (1.0 + th)
                gp[j, :, cs] = half + (0.5 * v) * (1.0 - th * th) * (
                    SCALE + (3.0 * SCALE * CUBIC) * v2
                )
                act = (v * half).astype(jnp.bfloat16)
                hb[d, :, cs] = act
                part = jnp.dot(act, wbuf[d, cs, :], preferred_element_type=jnp.float32)
                total = part if total is None else total + part
            y = (ub[...] + total).astype(jnp.bfloat16)
            yb[j] = y
            for buf, hbm, at in ((uh, uh_hbm, j), (gp, gp_hbm, j), (inv_b, inv_hbm, j), (hb, h_hbm, d)):
                copies.append(pltpu.make_async_copy(buf.at[at], hbm.at[at], osem.at[len(copies)]))
                copies[-1].start()
        y_ref[...] = yb[GROUP - 1]
        if towers:
            copies.append(pltpu.make_async_copy(yb, ys_hbm, osem.at[len(copies)]))
            copies[-1].start()
        for copy in copies:
            copy.wait()


def forward_stage(stage, skip, towers, flags, x, weights, par, k, h):
    rows, channels = x.shape
    f32, bf = jnp.float32, jnp.bfloat16
    wide = (GROUP, rows, channels)
    thin = (GROUP, rows, 128)
    out_shape = [
        jax.ShapeDtypeStruct((rows, channels), bf),
        jax.ShapeDtypeStruct(wide, f32),
        jax.ShapeDtypeStruct(wide, f32),
        jax.ShapeDtypeStruct(thin, f32),
        jax.ShapeDtypeStruct(wide, bf),
    ]
    out_specs = [VM, ANY, ANY, ANY, ANY]
    if towers:
        out_shape.append(jax.ShapeDtypeStruct(wide, bf))
        out_specs.append(ANY)
    args = [flags, x, *weights, par]
    in_specs = [SM, VM, ANY, ANY, ANY, ANY, VM]
    if skip:
        args.append(k)
        in_specs.append(VM)
    args.append(h)
    in_specs.append(ANY)
    return pl.pallas_call(
        functools.partial(forward_kernel, stage, skip, towers),
        out_shape=out_shape,
        in_specs=in_specs,
        out_specs=out_specs,
        scratch_shapes=[
            pltpu.VMEM((GROUP, channels, channels), bf),
            pltpu.VMEM((rows, channels), f32),
            pltpu.VMEM(wide, f32),
            pltpu.VMEM(wide, f32),
            pltpu.VMEM(thin, f32),
            pltpu.VMEM(wide, bf),
            pltpu.VMEM(wide, bf),
            pltpu.SemaphoreType.DMA((GROUP,)),
            pltpu.SemaphoreType.DMA((4 * GROUP + 1,)),
        ],
        input_output_aliases={len(args) - 1: 4},
        compiler_params=PARAMS,
        name=f"ahead{stage}",
    )(*args)


def backward_kernel(stage, last, first, flags, g_ref, w0, w1, w2, w3, par_ref, uh_hbm, gp_hbm, inv_hbm, *rest):
    rest = list(rest)
    k_ref = rest.pop(0) if first else None
    rest.pop(0)
    e_hbm = rest.pop(0)
    dx_ref = None if first else rest.pop(0)
    gk_hbm = rest.pop(0) if last else None
    wbuf, gb, mb, uh, gp, inv_b, eb, db, wsem, ssem, osem = rest
    channels = g_ref.shape[1]
    member = flags[1]

    @pl.when((flags[0] == stage) & (member < MICROS))
    def _():
        order = list(reversed(range(GROUP)))
        reads = {}
        for j in order:
            start_weights(member, [j], (w0, w1, w2, w3), wbuf, wsem)
            reads[j] = [
                pltpu.make_async_copy(hbm.at[j], buf.at[j], ssem.at[3 * j + i])
                for i, (hbm, buf) in enumerate(((uh_hbm, uh), (gp_hbm, gp), (inv_hbm, inv_b)))
            ]
            for read in reads[j]:
                read.start()
        copies = []
        for j in order:
            d = jnp.bitwise_xor(member, j)
            source = g_ref if j == GROUP - 1 else db.at[j + 1]
            for cs in chunks_of(channels):
                g = source[:, cs].astype(jnp.float32)
                if first:
                    g = g + k_ref[j, :, cs].astype(jnp.float32)
                gb[:, cs] = g
                eb[d, :, cs] = g.astype(jnp.bfloat16)
            copies.append(pltpu.make_async_copy(eb.at[d], e_hbm.at[d], osem.at[len(copies)]))
            copies[-1].start()
            pltpu.make_async_copy(w0, wbuf.at[d], wsem.at[d]).wait()
            for read in reads[j]:
                read.wait()
            if first and j == 0:
                continue
            e = eb[d]
            dots = None
            for cs in chunks_of(channels):
                da = lax.dot_general(
                    e, wbuf[d, cs, :], (((1,), (1,)), ((), ())), preferred_element_type=jnp.float32
                )
                dv = da * gp[j, :, cs]
                dn = (
                    par_ref[d, 0:1, cs] * row_after(dv)
                    + par_ref[d, 1:2, cs] * dv
                    + par_ref[d, 2:3, cs] * row_before(dv)
                )
                m = dn * par_ref[d, 3:4, cs]
                mb[:, cs] = m
                part = jnp.sum(m * uh[j, :, cs], axis=-1, keepdims=True)
                dots = part if dots is None else dots + part
            mean = dots * (1.0 / channels)
            inv = inv_b[j, :, 0:1]
            for cs in chunks_of(channels):
                du = inv * (mb[:, cs] - uh[j, :, cs] * mean)
                db[j, :, cs] = (gb[:, cs] + du).astype(jnp.bfloat16)
        if not first:
            dx_ref[...] = db[0]
        if last:
            copies.append(pltpu.make_async_copy(db, gk_hbm, osem.at[len(copies)]))
            copies[-1].start()
        for copy in copies:
            copy.wait()


def backward_stage(stage, last, first, flags, g, weights, par, state, k, e):
    rows, channels = g.shape
    f32, bf = jnp.float32, jnp.bfloat16
    wide = (GROUP, rows, channels)
    thin = (GROUP, rows, 128)
    args = [flags, g, *weights, par, *state]
    in_specs = [SM, VM, ANY, ANY, ANY, ANY, VM, ANY, ANY, ANY]
    if first:
        args.append(k)
        in_specs.append(VM)
    args.append(e)
    in_specs.append(ANY)
    out_shape = [jax.ShapeDtypeStruct(wide, bf)]
    out_specs = [ANY]
    if not first:
        out_shape.append(jax.ShapeDtypeStruct((rows, channels), bf))
        out_specs.append(VM)
    if last:
        out_shape.append(jax.ShapeDtypeStruct(wide, bf))
        out_specs.append(ANY)
    return pl.pallas_call(
        functools.partial(backward_kernel, stage, last, first),
        out_shape=out_shape,
        in_specs=in_specs,
        out_specs=out_specs,
        scratch_shapes=[
            pltpu.VMEM((GROUP, channels, channels), bf),
            pltpu.VMEM((rows, channels), f32),
            pltpu.VMEM((rows, channels), f32),
            pltpu.VMEM(wide, f32),
            pltpu.VMEM(wide, f32),
            pltpu.VMEM(thin, f32),
            pltpu.VMEM(wide, bf),
            pltpu.VMEM(wide, bf),
            pltpu.SemaphoreType.DMA((GROUP,)),
            pltpu.SemaphoreType.DMA((3 * GROUP,)),
            pltpu.SemaphoreType.DMA((GROUP + 1,)),
        ],
        input_output_aliases={len(args) - 1: 0},
        compiler_params=PARAMS,
        name=f"behind{stage}",
    )(*args)


def encode_bases(base_rows, embed_table):
    one_hot = (base_rows[:, :, None] == jnp.arange(4, dtype=jnp.int32)).astype(jnp.bfloat16)
    one_hot = one_hot.reshape(base_rows.shape[0], -1)
    return jnp.dot(one_hot, embed_table, preferred_element_type=jnp.float32).astype(jnp.bfloat16)


def swapped(block, distance, count):
    return lax.ppermute(block, "pipe", [(i, i ^ distance) for i in range(count)])


def shifted(block, stage, to_stage):
    pairs = [(GROUP * stage + i, GROUP * to_stage + i) for i in range(MICROS)]
    return lax.ppermute(block, "pipe", pairs)


def traded(block, distance, count):
    pairs = [(i, i ^ distance) for i in range(count) if i % GROUP < MICROS]
    return lax.ppermute(block[distance], "pipe", pairs)


def shards(base_ids, embed_table, segment_weights, conv_taps, norm_gains, cotangent):
    count = lax.axis_size("pipe")
    replicas = lax.axis_size("dp")
    stages = count // GROUP
    position = lax.axis_index("pipe")
    member = position % GROUP
    flags = jnp.stack([position // GROUP, member]).astype(jnp.int32)
    micro = jnp.minimum(member, MICROS - 1)
    weight = segment_weights[0]
    channels = weight.shape[1]
    row_count = base_ids.shape[2]
    half = channels // 2

    own = jnp.concatenate([conv_taps[0], norm_gains, jnp.zeros((4, channels), jnp.float32)])
    across = [swapped(weight[:half], 2, count), swapped(weight[half:], 2, count)]
    beside = swapped(weight, 1, count)
    par = jnp.stack([own] + [swapped(own, d, count) for d in range(1, GROUP)])
    corner = [swapped(part, 1, count) for part in across]
    weights = (weight, beside, jnp.concatenate(across), jnp.concatenate(corner))

    x = encode_bases(base_ids[0, micro], embed_table)
    wide = (GROUP, row_count, channels)
    h = jnp.zeros(wide, jnp.bfloat16)
    e = jnp.zeros(wide, jnp.bfloat16)
    states, k = [], None
    for stage in range(stages):
        skip, towers = stage == stages - 1, stage == 0
        outs = forward_stage(stage, skip, towers, flags, x, weights, par, k, h)
        states.append(outs[1:4])
        h = outs[4]
        if towers:
            k = shifted(outs[5], 0, stages - 1)
        if stage < stages - 1:
            x = shifted(outs[0], stage, stage + 1)

    g = cotangent[0, micro]
    returned = None
    for stage in reversed(range(stages)):
        last, first = stage == stages - 1, stage == 0
        outs = backward_stage(stage, last, first, flags, g, weights, par, states[stage], returned, e)
        e = outs[0]
        if last:
            returned = shifted(outs[2], stages - 1, 0)
            h, e = lax.optimization_barrier((h, e))
            acts = jnp.concatenate([h[0]] + [traded(h, d, count) for d in range(1, GROUP)])
        if stage > 0:
            g = shifted(outs[1], stage, stage - 1)
    errors = jnp.concatenate([e[0]] + [traded(e, d, count) for d in range(1, GROUP)])

    terms = lax.dot_general(acts, errors, (((0,), (0,)), ((), ())), preferred_element_type=jnp.float32)
    pieces = terms.astype(jnp.bfloat16).reshape(replicas, channels // replicas, channels)
    pieces = lax.all_to_all(pieces, "dp", 0, 0)
    factor = 1.0 / math.sqrt(replicas * MICROS * row_count)
    piece = jnp.sum(pieces.astype(jnp.float32), axis=0) * factor
    piece = jnp.broadcast_to(piece.astype(jnp.bfloat16)[None], pieces.shape)
    whole = lax.all_to_all(piece, "dp", 0, 0)
    return whole.reshape(1, channels, channels).astype(jnp.float32)


def solution(mesh):
    return jax.shard_map(
        shards,
        mesh=mesh,
        in_specs=(
            P("dp", None, None, None),
            P(),
            P("pipe", None, None),
            P("pipe", None, None),
            P("pipe", None),
            P("dp", None, None, None),
        ),
        out_specs=P("pipe", None, None),
        check_vma=False,
    )
```

```python
import functools
import math

import jax
import jax.numpy as jnp
from jax import lax
from jax.experimental import pallas as pl
from jax.experimental.pallas import tpu as pltpu
from jax.sharding import PartitionSpec as P

GROUP = 4
MICROS = 3
CHUNK = 256
ANY = pl.BlockSpec(memory_space=pl.ANY)
VM = pl.BlockSpec(memory_space=pltpu.VMEM)
SM = pl.BlockSpec(memory_space=pltpu.SMEM)
PARAMS = pltpu.CompilerParams(vmem_limit_bytes=24 * 1024 * 1024)
CUBIC = 0.044715
SCALE = math.sqrt(2.0 / math.pi)


def row_before(block):
    rows = lax.broadcasted_iota(jnp.int32, block.shape, 0)
    return jnp.where(rows == 0, 0.0, pltpu.roll(block, 1, 0))


def row_after(block):
    size = block.shape[0]
    rows = lax.broadcasted_iota(jnp.int32, block.shape, 0)
    return jnp.where(rows == size - 1, 0.0, pltpu.roll(block, size - 1, 0))


def chunks_of(channels):
    return [slice(c, c + CHUNK) for c in range(0, channels, CHUNK)]


def forward_kernel(stage, skip, towers, flags, x_ref, w_ref, par_ref, *rest):
    rest = list(rest)
    k_ref = rest.pop(0) if skip else None
    h_ref = rest.pop(0)
    y_ref, uh, gp, inv_b, hb = rest[:5]
    rest = rest[5:]
    ys = rest.pop(0) if towers else None
    (ub,) = rest
    channels = x_ref.shape[1]
    member = flags[1]
    active = (flags[0] == stage) & (member < MICROS)

    @pl.when(jnp.logical_not(active))
    def _():
        hb[...] = h_ref[...]

    @pl.when(active)
    def _():
        y = x_ref[...]
        for j in range(GROUP):
            d = jnp.bitwise_xor(member, j)
            squares = None
            for cs in chunks_of(channels):
                u = y[:, cs].astype(jnp.float32)
                if skip:
                    u = u + k_ref[j, :, cs].astype(jnp.float32)
                ub[:, cs] = u
                part = jnp.sum(u * u, axis=-1, keepdims=True)
                squares = part if squares is None else squares + part
            inv = lax.rsqrt(squares * (1.0 / channels) + 1e-06)
            inv_b[j] = jnp.broadcast_to(inv, inv_b.shape[1:])
            total = None
            for cs in chunks_of(channels):
                unit = ub[:, cs] * inv
                uh[j, :, cs] = unit
                n = unit * par_ref[j, 3:4, cs]
                v = (
                    par_ref[j, 0:1, cs] * row_before(n)
                    + par_ref[j, 1:2, cs] * n
                    + par_ref[j, 2:3, cs] * row_after(n)
                )
                v2 = v * v
                th = jnp.tanh(v * (SCALE + (SCALE * CUBIC) * v2))
                half = 0.5 * (1.0 + th)
                gp[j, :, cs] = half + (0.5 * v) * (1.0 - th * th) * (
                    SCALE + (3.0 * SCALE * CUBIC) * v2
                )
                act = (v * half).astype(jnp.bfloat16)
                hb[d, :, cs] = act
                part = jnp.dot(act, w_ref[j, cs, :], preferred_element_type=jnp.float32)
                total = part if total is None else total + part
            y = (ub[...] + total).astype(jnp.bfloat16)
            if towers:
                ys[j] = y
        y_ref[...] = y


def kept(shape, kind):
    return pltpu.VMEM(shape, kind)


def held(*arrays):
    return [pltpu.with_memory_space_constraint(a, pltpu.VMEM) for a in arrays]


def forward_stage(stage, skip, towers, flags, x, weights, par, k, h):
    rows, channels = x.shape
    f32, bf = jnp.float32, jnp.bfloat16
    wide = (GROUP, rows, channels)
    thin = (GROUP, rows, 128)
    out_shape = [
        kept((rows, channels), bf),
        kept(wide, f32),
        kept(wide, f32),
        kept(thin, f32),
        kept(wide, bf),
    ]
    if towers:
        out_shape.append(kept(wide, bf))
    args = [x, weights, par]
    if skip:
        args.append(k)
    args.append(h)
    args = [flags] + held(*args)
    return pl.pallas_call(
        functools.partial(forward_kernel, stage, skip, towers),
        out_shape=out_shape,
        in_specs=[SM] + [VM] * (len(args) - 1),
        out_specs=[VM] * len(out_shape),
        scratch_shapes=[pltpu.VMEM((rows, channels), f32)],
        input_output_aliases={len(args) - 1: 4},
        compiler_params=PARAMS,
        name=f"ahead{stage}",
    )(*args)


def backward_kernel(stage, last, first, flags, g_ref, w_ref, par_ref, uh, gp, inv_b, *rest):
    rest = list(rest)
    k_ref = rest.pop(0) if first else None
    e_ref = rest.pop(0)
    eb = rest.pop(0)
    dx_ref = None if first else rest.pop(0)
    gk_ref = rest.pop(0) if last else None
    gb, mb = rest
    channels = g_ref.shape[1]
    member = flags[1]
    active = (flags[0] == stage) & (member < MICROS)

    @pl.when(jnp.logical_not(active))
    def _():
        eb[...] = e_ref[...]

    @pl.when(active)
    def _():
        dx = g_ref[...]
        for j in reversed(range(GROUP)):
            d = jnp.bitwise_xor(member, j)
            for cs in chunks_of(channels):
                g = dx[:, cs].astype(jnp.float32)
                if first:
                    g = g + k_ref[j, :, cs].astype(jnp.float32)
                gb[:, cs] = g
            e = gb[...].astype(jnp.bfloat16)
            eb[d] = e
            if first and j == 0:
                continue
            dots = None
            for cs in chunks_of(channels):
                da = lax.dot_general(
                    e, w_ref[j, cs, :], (((1,), (1,)), ((), ())), preferred_element_type=jnp.float32
                )
                dv = da * gp[j, :, cs]
                dn = (
                    par_ref[j, 0:1, cs] * row_after(dv)
                    + par_ref[j, 1:2, cs] * dv
                    + par_ref[j, 2:3, cs] * row_before(dv)
                )
                m = dn * par_ref[j, 3:4, cs]
                mb[:, cs] = m
                part = jnp.sum(m * uh[j, :, cs], axis=-1, keepdims=True)
                dots = part if dots is None else dots + part
            mean = dots * (1.0 / channels)
            inv = inv_b[j, :, 0:1]
            dx = (gb[...] + inv * (mb[...] - uh[j] * mean)).astype(jnp.bfloat16)
            if last:
                gk_ref[j] = dx
        if not first:
            dx_ref[...] = dx


def backward_stage(stage, last, first, flags, g, weights, par, state, k, e):
    rows, channels = g.shape
    f32, bf = jnp.float32, jnp.bfloat16
    wide = (GROUP, rows, channels)
    args = [g, weights, par, *state]
    if first:
        args.append(k)
    args.append(e)
    args = [flags] + held(*args)
    out_shape = [kept(wide, bf)]
    if not first:
        out_shape.append(kept((rows, channels), bf))
    if last:
        out_shape.append(kept(wide, bf))
    return pl.pallas_call(
        functools.partial(backward_kernel, stage, last, first),
        out_shape=out_shape,
        in_specs=[SM] + [VM] * (len(args) - 1),
        out_specs=[VM] * len(out_shape),
        scratch_shapes=[pltpu.VMEM((rows, channels), f32)] * 2,
        input_output_aliases={len(args) - 1: 0},
        compiler_params=PARAMS,
        name=f"behind{stage}",
    )(*args)


def encode_bases(base_rows, embed_table):
    one_hot = (base_rows[:, :, None] == jnp.arange(4, dtype=jnp.int32)).astype(jnp.bfloat16)
    one_hot = one_hot.reshape(base_rows.shape[0], -1)
    return jnp.dot(one_hot, embed_table, preferred_element_type=jnp.float32).astype(jnp.bfloat16)


def swapped(block, distance, count):
    return lax.ppermute(block, "pipe", [(i, i ^ distance) for i in range(count)])


def pack_kernel(places, flags, *rest):
    parts, out, sems = rest[: len(places)], rest[-2], rest[-1]
    copies = []
    for i, ((d, row), part) in enumerate(zip(places, parts)):
        slot = jnp.bitwise_xor(flags[1], d)
        target = out.at[slot, pl.ds(row, part.shape[0]), :]
        copies.append(pltpu.make_async_copy(part, target, sems.at[i]))
        copies[-1].start()
    for copy in copies:
        copy.wait()


def packed(stack, flags, items):
    places = [(d, row) for d, row, _ in items]
    parts = [part for _, _, part in items]
    channels = parts[0].shape[1]
    args, specs, aliases = [flags] + parts, [SM] + [ANY] * len(parts), {}
    if stack is not None:
        aliases = {len(args): 0}
        args += held(stack)
        specs.append(ANY)
    return pl.pallas_call(
        functools.partial(pack_kernel, places),
        out_shape=kept((GROUP, channels, channels), jnp.bfloat16),
        in_specs=specs,
        out_specs=ANY,
        scratch_shapes=[pltpu.SemaphoreType.DMA((len(parts),))],
        input_output_aliases=aliases,
        compiler_params=PARAMS,
        name="packed",
    )(*args)


def placed(stack, parts, member, row=0):
    for d, part in enumerate(parts):
        if part is not None:
            slot = jnp.bitwise_xor(member, d)
            stack = lax.dynamic_update_slice(stack, part[None], (slot, row, 0))
    return stack


def shifted(block, stage, to_stage):
    pairs = [(GROUP * stage + i, GROUP * to_stage + i) for i in range(MICROS)]
    return lax.ppermute(block, "pipe", pairs)


def traded(block, distance, count):
    pairs = [(i, i ^ distance) for i in range(count) if i % GROUP < MICROS]
    return lax.ppermute(block[distance], "pipe", pairs)


def shards(base_ids, embed_table, segment_weights, conv_taps, norm_gains, cotangent):
    count = lax.axis_size("pipe")
    replicas = lax.axis_size("dp")
    stages = count // GROUP
    position = lax.axis_index("pipe")
    member = position % GROUP
    flags = jnp.stack([position // GROUP, member]).astype(jnp.int32)
    micro = jnp.minimum(member, MICROS - 1)
    weight = segment_weights[0]
    channels = weight.shape[1]
    row_count = base_ids.shape[2]
    half = channels // 2

    own = jnp.concatenate([conv_taps[0], norm_gains, jnp.zeros((4, channels), jnp.float32)])
    across = [swapped(weight[:half], 2, count), swapped(weight[half:], 2, count)]
    beside = swapped(weight, 1, count)
    par = placed(
        jnp.zeros((GROUP,) + own.shape, jnp.float32),
        [own] + [swapped(own, d, count) for d in range(1, GROUP)],
        member,
    )
    corner = [swapped(part, 1, count) for part in across]
    weights = packed(None, flags, [(0, 0, weight), (1, 0, beside)])
    weights = packed(weights, flags, [(2, 0, across[0]), (3, 0, corner[0]), (2, half, across[1])])
    weights = packed(weights, flags, [(3, half, corner[1])])

    x = encode_bases(base_ids[0, micro], embed_table)
    wide = (GROUP, row_count, channels)
    h = jnp.zeros(wide, jnp.bfloat16)
    e = jnp.zeros(wide, jnp.bfloat16)
    states, k = [], None
    for stage in range(stages):
        skip, towers = stage == stages - 1, stage == 0
        outs = forward_stage(stage, skip, towers, flags, x, weights, par, k, h)
        states.append(outs[1:4])
        h = outs[4]
        if stage < stages - 1:
            x = shifted(outs[0], stage, stage + 1)
        if towers:
            x, tower = lax.optimization_barrier((x, outs[5]))
            k = shifted(tower, 0, stages - 1)

    g = cotangent[0, micro]
    returned = None
    for stage in reversed(range(stages)):
        last, first = stage == stages - 1, stage == 0
        outs = backward_stage(stage, last, first, flags, g, weights, par, states[stage], returned, e)
        e = outs[0]
        if stage > 0:
            g = shifted(outs[1], stage, stage - 1)
        if last:
            g, skip_grad = lax.optimization_barrier((g, outs[2]))
            returned = shifted(skip_grad, stages - 1, 0)
        if stage == stages - 2:
            h, e = lax.optimization_barrier((h, e))
            acts = jnp.concatenate([h[0]] + [traded(h, d, count) for d in range(1, GROUP)])
    errors = jnp.concatenate([e[0]] + [traded(e, d, count) for d in range(1, GROUP)])

    terms = lax.dot_general(acts, errors, (((0,), (0,)), ((), ())), preferred_element_type=jnp.float32)
    pieces = terms.astype(jnp.bfloat16).reshape(replicas, channels // replicas, channels)
    pieces = lax.all_to_all(pieces, "dp", 0, 0)
    factor = 1.0 / math.sqrt(replicas * MICROS * row_count)
    piece = jnp.sum(pieces.astype(jnp.float32), axis=0) * factor
    piece = jnp.broadcast_to(piece.astype(jnp.bfloat16)[None], pieces.shape)
    whole = lax.all_to_all(piece, "dp", 0, 0)
    return whole.reshape(1, channels, channels).astype(jnp.float32)


def solution(mesh):
    return jax.shard_map(
        shards,
        mesh=mesh,
        in_specs=(
            P("dp", None, None, None),
            P(),
            P("pipe", None, None),
            P("pipe", None, None),
            P("pipe", None),
            P("dp", None, None, None),
        ),
        out_specs=P("pipe", None, None),
        check_vma=False,
    )
```

```python
import functools
import math

import jax
import jax.numpy as jnp
from jax import lax
from jax.experimental import pallas as pl
from jax.experimental.pallas import tpu as pltpu
from jax.sharding import Mesh
from jax.sharding import PartitionSpec as P

GROUP = 4
MICROS = 3
CHUNK = 256
PIPE = ("g", "q")
ANY = pl.BlockSpec(memory_space=pl.ANY)
VM = pl.BlockSpec(memory_space=pltpu.VMEM)
SM = pl.BlockSpec(memory_space=pltpu.SMEM)
PARAMS = pltpu.CompilerParams(vmem_limit_bytes=4 * 1024 * 1024)
CUBIC = 0.044715
SCALE = math.sqrt(2.0 / math.pi)


def row_before(block):
    rows = lax.broadcasted_iota(jnp.int32, block.shape, 0)
    return jnp.where(rows == 0, 0.0, pltpu.roll(block, 1, 0))


def row_after(block):
    size = block.shape[0]
    rows = lax.broadcasted_iota(jnp.int32, block.shape, 0)
    return jnp.where(rows == size - 1, 0.0, pltpu.roll(block, size - 1, 0))


def chunks_of(channels):
    return [slice(c, c + CHUNK) for c in range(0, channels, CHUNK)]


def forward_kernel(stage, skip, towers, flags, x_ref, w_ref, par_ref, *rest):
    rest = list(rest)
    k_ref = rest.pop(0) if skip else None
    h_ref = rest.pop(0)
    y_ref, uh, gp, inv_b, hb = rest[:5]
    rest = rest[5:]
    ys = rest.pop(0) if towers else None
    (ub,) = rest
    channels = x_ref.shape[1]
    member = flags[1]
    active = (flags[0] == stage) & (member < MICROS)

    @pl.when(jnp.logical_not(active))
    def _():
        hb[...] = h_ref[...]

    @pl.when(active)
    def _():
        y = x_ref[...]
        for j in range(GROUP):
            squares = None
            for cs in chunks_of(channels):
                u = y[:, cs].astype(jnp.float32)
                if skip:
                    u = u + k_ref[j, :, cs].astype(jnp.float32)
                ub[:, cs] = u
                part = jnp.sum(u * u, axis=-1, keepdims=True)
                squares = part if squares is None else squares + part
            inv = lax.rsqrt(squares * (1.0 / channels) + 1e-06)
            inv_b[j] = jnp.broadcast_to(inv, inv_b.shape[1:])
            total = None
            for cs in chunks_of(channels):
                unit = ub[:, cs] * inv
                uh[j, :, cs] = unit
                n = unit * par_ref[j, 3:4, cs]
                v = (
                    par_ref[j, 0:1, cs] * row_before(n)
                    + par_ref[j, 1:2, cs] * n
                    + par_ref[j, 2:3, cs] * row_after(n)
                )
                v2 = v * v
                th = jnp.tanh(v * (SCALE + (SCALE * CUBIC) * v2))
                half = 0.5 * (1.0 + th)
                gp[j, :, cs] = half + (0.5 * v) * (1.0 - th * th) * (
                    SCALE + (3.0 * SCALE * CUBIC) * v2
                )
                act = (v * half).astype(jnp.bfloat16)
                hb[j, :, cs] = act
                part = jnp.dot(act, w_ref[j, cs, :], preferred_element_type=jnp.float32)
                total = part if total is None else total + part
            y = (ub[...] + total).astype(jnp.bfloat16)
            if towers:
                ys[j] = y
        y_ref[...] = y


def kept(shape, kind):
    return pltpu.VMEM(shape, kind)


def held(*arrays):
    return [pltpu.with_memory_space_constraint(a, pltpu.VMEM) for a in arrays]


def forward_stage(stage, skip, towers, flags, x, weights, par, k, h):
    rows, channels = x.shape
    f32, bf = jnp.float32, jnp.bfloat16
    wide = (GROUP, rows, channels)
    thin = (GROUP, rows, 128)
    out_shape = [
        kept((rows, channels), bf),
        kept(wide, f32),
        kept(wide, f32),
        kept(thin, f32),
        kept(wide, bf),
    ]
    if towers:
        out_shape.append(kept(wide, bf))
    args = [x, weights, par]
    if skip:
        args.append(k)
    args.append(h)
    args = [flags] + held(*args)
    return pl.pallas_call(
        functools.partial(forward_kernel, stage, skip, towers),
        out_shape=out_shape,
        in_specs=[SM] + [VM] * (len(args) - 1),
        out_specs=[VM] * len(out_shape),
        scratch_shapes=[pltpu.VMEM((rows, channels), f32)],
        input_output_aliases={len(args) - 1: 4},
        compiler_params=PARAMS,
        name=f"ahead{stage}",
    )(*args)


def backward_kernel(stage, last, first, flags, g_ref, w_ref, par_ref, uh, gp, inv_b, *rest):
    rest = list(rest)
    k_ref = rest.pop(0) if first else None
    e_ref = rest.pop(0)
    eb = rest.pop(0)
    dx_ref = None if first else rest.pop(0)
    gk_ref = rest.pop(0) if last else None
    gb, mb = rest
    channels = g_ref.shape[1]
    member = flags[1]
    active = (flags[0] == stage) & (member < MICROS)

    @pl.when(jnp.logical_not(active))
    def _():
        eb[...] = e_ref[...]

    @pl.when(active)
    def _():
        dx = g_ref[...]
        for j in reversed(range(GROUP)):
            for cs in chunks_of(channels):
                g = dx[:, cs].astype(jnp.float32)
                if first:
                    g = g + k_ref[j, :, cs].astype(jnp.float32)
                gb[:, cs] = g
            e = gb[...].astype(jnp.bfloat16)
            for i in range(eb.shape[0]):
                eb[i, j] = e[:, i * eb.shape[3] : (i + 1) * eb.shape[3]]
            if first and j == 0:
                continue
            dots = None
            for cs in chunks_of(channels):
                da = lax.dot_general(
                    e, w_ref[j, cs, :], (((1,), (1,)), ((), ())), preferred_element_type=jnp.float32
                )
                dv = da * gp[j, :, cs]
                dn = (
                    par_ref[j, 0:1, cs] * row_after(dv)
                    + par_ref[j, 1:2, cs] * dv
                    + par_ref[j, 2:3, cs] * row_before(dv)
                )
                m = dn * par_ref[j, 3:4, cs]
                mb[:, cs] = m
                part = jnp.sum(m * uh[j, :, cs], axis=-1, keepdims=True)
                dots = part if dots is None else dots + part
            mean = dots * (1.0 / channels)
            inv = inv_b[j, :, 0:1]
            dx = (gb[...] + inv * (mb[...] - uh[j] * mean)).astype(jnp.bfloat16)
            if last:
                gk_ref[j] = dx
        if not first:
            dx_ref[...] = dx


def backward_stage(stage, last, first, flags, g, weights, par, state, k, e):
    rows, channels = g.shape
    f32, bf = jnp.float32, jnp.bfloat16
    wide = (GROUP, rows, channels)
    args = [g, weights, par, *state]
    if first:
        args.append(k)
    args.append(e)
    args = [flags] + held(*args)
    out_shape = [kept(e.shape, bf)]
    if not first:
        out_shape.append(kept((rows, channels), bf))
    if last:
        out_shape.append(kept(wide, bf))
    return pl.pallas_call(
        functools.partial(backward_kernel, stage, last, first),
        out_shape=out_shape,
        in_specs=[SM] + [VM] * (len(args) - 1),
        out_specs=[VM] * len(out_shape),
        scratch_shapes=[pltpu.VMEM((rows, channels), f32)] * 2,
        input_output_aliases={len(args) - 1: 0},
        compiler_params=PARAMS,
        name=f"behind{stage}",
    )(*args)


def encode_bases(base_rows, embed_table):
    one_hot = (base_rows[:, :, None] == jnp.arange(4, dtype=jnp.int32)).astype(jnp.bfloat16)
    one_hot = one_hot.reshape(base_rows.shape[0], -1)
    return jnp.dot(one_hot, embed_table, preferred_element_type=jnp.float32).astype(jnp.bfloat16)


def swapped(block, distance):
    pairs = [(i, i ^ distance) for i in range(lax.axis_size(PIPE))]
    return lax.ppermute(block, PIPE, pairs)


def pack_kernel(places, flags, *rest):
    parts, out, sems = rest[: len(places)], rest[-2], rest[-1]
    copies = []
    for i, ((d, row), part) in enumerate(zip(places, parts)):
        slot = jnp.bitwise_xor(flags[1], d)
        target = out.at[slot, pl.ds(row, part.shape[0]), :]
        copies.append(pltpu.make_async_copy(part, target, sems.at[i]))
        copies[-1].start()
    for copy in copies:
        copy.wait()


def packed(stack, flags, items):
    places = [(d, row) for d, row, _ in items]
    parts = [part for _, _, part in items]
    channels = parts[0].shape[1]
    args, specs, aliases = [flags] + parts, [SM] + [ANY] * len(parts), {}
    if stack is not None:
        aliases = {len(args): 0}
        args += held(stack)
        specs.append(ANY)
    return pl.pallas_call(
        functools.partial(pack_kernel, places),
        out_shape=kept((GROUP, channels, channels), jnp.bfloat16),
        in_specs=specs,
        out_specs=ANY,
        scratch_shapes=[pltpu.SemaphoreType.DMA((len(parts),))],
        input_output_aliases=aliases,
        compiler_params=PARAMS,
        name="packed",
    )(*args)


def placed(stack, parts, member, row=0):
    for d, part in enumerate(parts):
        if part is not None:
            slot = jnp.bitwise_xor(member, d)
            stack = lax.dynamic_update_slice(stack, part[None], (slot, row, 0))
    return stack


def shifted(block, stage, to_stage):
    pairs = [(GROUP * stage + i, GROUP * to_stage + i) for i in range(MICROS)]
    return lax.ppermute(block, PIPE, pairs)


def gathered(h, member, across_count):
    group = jnp.zeros(h.shape, h.dtype)
    own = lax.dynamic_index_in_dim(h, member, 0, keepdims=True)
    group = lax.dynamic_update_slice(group, own, (member, 0, 0))
    for d in range(1, GROUP):
        slot = jnp.bitwise_xor(member, d)
        pairs = [(i, i ^ d) for i in range(lax.axis_size(PIPE)) if i % GROUP < MICROS]
        sent = lax.dynamic_index_in_dim(h, slot, 0, keepdims=True)
        group = lax.dynamic_update_slice(group, lax.ppermute(sent, PIPE, pairs), (slot, 0, 0))
    group = group.reshape(1, -1, h.shape[2])
    here = lax.axis_index("x")
    acts = jnp.zeros((across_count,) + group.shape[1:], h.dtype)
    acts = lax.dynamic_update_slice(acts, group, (here, 0, 0))
    for shift in range(1, across_count):
        pairs = [(i, (i + shift) % across_count) for i in range(across_count)]
        slot = (here - shift) % across_count
        acts = lax.dynamic_update_slice(acts, lax.ppermute(group, "x", pairs), (slot, 0, 0))
    return acts.reshape(-1, h.shape[2])


def shards(base_ids, embed_table, segment_weights, conv_taps, norm_gains, cotangent):
    stages = lax.axis_size("g")
    down, across_count = lax.axis_size("y"), lax.axis_size("x")
    member = lax.axis_index("q")
    flags = jnp.stack([lax.axis_index("g"), member]).astype(jnp.int32)
    micro = jnp.minimum(member, MICROS - 1)
    weight = segment_weights[0]
    channels = weight.shape[1]
    row_count = base_ids.shape[2]
    block = channels // across_count
    bf = jnp.bfloat16

    across = swapped(weight, 2)
    x = encode_bases(base_ids[0, micro], embed_table)
    later, x = lax.optimization_barrier((weight, x))
    beside = swapped(later, 1)
    own = jnp.concatenate([conv_taps[0], norm_gains, jnp.zeros((4, channels), jnp.float32)])
    own, beside = lax.optimization_barrier((own, beside))
    par = placed(
        jnp.zeros((GROUP,) + own.shape, jnp.float32),
        [own] + [swapped(own, d) for d in range(1, GROUP)],
        member,
    )
    weights = packed(None, flags, [(0, 0, weight), (1, 0, beside)])
    across, weights, par, x = lax.optimization_barrier((across, weights, par, x))
    corner = swapped(across, 1)
    weights = packed(weights, flags, [(2, 0, across)])
    weights = packed(weights, flags, [(3, 0, corner)])
    h = jnp.zeros((GROUP, row_count, channels), bf)
    e = jnp.zeros((across_count, GROUP, row_count, block), bf)
    states, k = [], None
    for stage in range(stages):
        skip, towers = stage == stages - 1, stage == 0
        outs = forward_stage(stage, skip, towers, flags, x, weights, par, k, h)
        states.append(outs[1:4])
        h = outs[4]
        if stage < stages - 1:
            x = shifted(outs[0], stage, stage + 1)
        if towers:
            x, tower = lax.optimization_barrier((x, outs[5]))
            k = shifted(tower, 0, stages - 1)

    g = cotangent[0, micro]
    returned = None
    for stage in reversed(range(stages)):
        last, first = stage == stages - 1, stage == 0
        outs = backward_stage(stage, last, first, flags, g, weights, par, states[stage], returned, e)
        e = outs[0]
        if stage > 0:
            g = shifted(outs[1], stage, stage - 1)
        if last:
            g, skip_grad = lax.optimization_barrier((g, outs[2]))
            returned = shifted(skip_grad, stages - 1, 0)
        if stage == stages - 2:
            h, e = lax.optimization_barrier((h, e))
            acts = gathered(h, member, across_count)
        if stage == 1:
            acts, e = lax.optimization_barrier((acts, e))
    errors = lax.all_to_all(e.reshape(-1, row_count, block), ("x", "q"), 0, 0).reshape(-1, block)

    turned = lax.dot_general(errors, acts, (((0,), (0,)), ((), ())), preferred_element_type=jnp.float32)
    pieces = lax.all_to_all(turned.astype(bf).reshape(down, block // down, channels), "y", 0, 0)
    factor = 1.0 / math.sqrt(down * across_count * MICROS * row_count)
    piece = (jnp.sum(pieces.astype(jnp.float32), axis=0) * factor).astype(bf)
    piece = jnp.broadcast_to(piece, (across_count * down,) + piece.shape)
    whole = lax.all_to_all(piece, ("x", "y"), 0, 0).reshape(channels, channels)
    return whole.T.astype(jnp.float32)[None]


def solution(mesh):
    replicas, _ = mesh.devices.shape
    shape = (replicas // math.gcd(4, replicas), math.gcd(4, replicas), -1, GROUP)
    grid = Mesh(mesh.devices.reshape(shape), ("y", "x", "g", "q"))
    windows = P(("y", "x"), None, None, None)
    return jax.shard_map(
        shards,
        mesh=grid,
        in_specs=(
            windows,
            P(),
            P(PIPE, None, None),
            P(PIPE, None, None),
            P(PIPE, None),
            windows,
        ),
        out_specs=P(PIPE, None, None),
        check_vma=False,
    )
```

```python
import functools
import math

import jax
import jax.numpy as jnp
from jax import lax
from jax.experimental import pallas as pl
from jax.experimental.pallas import tpu as pltpu
from jax.sharding import Mesh
from jax.sharding import PartitionSpec as P

GROUP = 4
MICROS = 3
CHUNK = 256
PIPE = ("g", "q")
ANY = pl.BlockSpec(memory_space=pl.ANY)
VM = pl.BlockSpec(memory_space=pltpu.VMEM)
SM = pl.BlockSpec(memory_space=pltpu.SMEM)
PARAMS = pltpu.CompilerParams(vmem_limit_bytes=4 * 1024 * 1024)
CUBIC = 0.044715
SCALE = math.sqrt(2.0 / math.pi)


def row_before(block):
    rows = lax.broadcasted_iota(jnp.int32, block.shape, 0)
    return jnp.where(rows == 0, 0.0, pltpu.roll(block, 1, 0))


def row_after(block):
    size = block.shape[0]
    rows = lax.broadcasted_iota(jnp.int32, block.shape, 0)
    return jnp.where(rows == size - 1, 0.0, pltpu.roll(block, size - 1, 0))


def chunks_of(channels):
    return [slice(c, c + CHUNK) for c in range(0, channels, CHUNK)]


def forward_kernel(stage, skip, towers, flags, x_ref, w_ref, par_ref, *rest):
    rest = list(rest)
    k_ref = rest.pop(0) if skip else None
    h_ref = rest.pop(0)
    y_ref, uh, gp, inv_b, hb = rest[:5]
    rest = rest[5:]
    ys = rest.pop(0) if towers else None
    (ub,) = rest
    channels = x_ref.shape[1]
    member = flags[1]
    active = (flags[0] == stage) & (member < MICROS)

    @pl.when(jnp.logical_not(active))
    def _():
        hb[...] = h_ref[...]

    @pl.when(active)
    def _():
        y = x_ref[...]
        for j in range(GROUP):
            d = jnp.bitwise_xor(member, j)
            squares = None
            for cs in chunks_of(channels):
                u = y[:, cs].astype(jnp.float32)
                if skip:
                    u = u + k_ref[j, :, cs].astype(jnp.float32)
                ub[:, cs] = u
                part = jnp.sum(u * u, axis=-1, keepdims=True)
                squares = part if squares is None else squares + part
            inv = lax.rsqrt(squares * (1.0 / channels) + 1e-06)
            inv_b[j] = jnp.broadcast_to(inv, inv_b.shape[1:])
            total = None
            for cs in chunks_of(channels):
                unit = ub[:, cs] * inv
                uh[j, :, cs] = unit
                n = unit * par_ref[j, 3:4, cs]
                v = (
                    par_ref[j, 0:1, cs] * row_before(n)
                    + par_ref[j, 1:2, cs] * n
                    + par_ref[j, 2:3, cs] * row_after(n)
                )
                v2 = v * v
                th = jnp.tanh(v * (SCALE + (SCALE * CUBIC) * v2))
                half = 0.5 * (1.0 + th)
                gp[j, :, cs] = half + (0.5 * v) * (1.0 - th * th) * (
                    SCALE + (3.0 * SCALE * CUBIC) * v2
                )
                act = (v * half).astype(jnp.bfloat16)
                hb[d, :, cs] = act
                part = jnp.dot(act, w_ref[j, cs, :], preferred_element_type=jnp.float32)
                total = part if total is None else total + part
            y = (ub[...] + total).astype(jnp.bfloat16)
            if towers:
                ys[j] = y
        y_ref[...] = y


def kept(shape, kind):
    return pltpu.VMEM(shape, kind)


def held(*arrays):
    return [pltpu.with_memory_space_constraint(a, pltpu.VMEM) for a in arrays]


def forward_stage(stage, skip, towers, flags, x, weights, par, k, h):
    rows, channels = x.shape
    f32, bf = jnp.float32, jnp.bfloat16
    wide = (GROUP, rows, channels)
    thin = (GROUP, rows, 128)
    out_shape = [
        kept((rows, channels), bf),
        kept(wide, f32),
        kept(wide, f32),
        kept(thin, f32),
        kept(wide, bf),
    ]
    if towers:
        out_shape.append(kept(wide, bf))
    args = [x, weights, par]
    if skip:
        args.append(k)
    args.append(h)
    args = [flags] + held(*args)
    return pl.pallas_call(
        functools.partial(forward_kernel, stage, skip, towers),
        out_shape=out_shape,
        in_specs=[SM] + [VM] * (len(args) - 1),
        out_specs=[VM] * len(out_shape),
        scratch_shapes=[pltpu.VMEM((rows, channels), f32)],
        input_output_aliases={len(args) - 1: 4},
        compiler_params=PARAMS,
        name=f"ahead{stage}",
    )(*args)


def backward_kernel(stage, last, first, flags, g_ref, w_ref, par_ref, uh, gp, inv_b, *rest):
    rest = list(rest)
    k_ref = rest.pop(0) if first else None
    e_ref = rest.pop(0)
    eb = rest.pop(0)
    dx_ref = None if first else rest.pop(0)
    gk_ref = rest.pop(0) if last else None
    gb, mb = rest
    channels = g_ref.shape[1]
    member = flags[1]
    active = (flags[0] == stage) & (member < MICROS)

    @pl.when(jnp.logical_not(active))
    def _():
        eb[...] = e_ref[...]

    @pl.when(active)
    def _():
        dx = g_ref[...]
        for j in reversed(range(GROUP)):
            for cs in chunks_of(channels):
                g = dx[:, cs].astype(jnp.float32)
                if first:
                    g = g + k_ref[j, :, cs].astype(jnp.float32)
                gb[:, cs] = g
            e = gb[...].astype(jnp.bfloat16)
            for i in range(eb.shape[0]):
                eb[i, j] = e[:, i * eb.shape[3] : (i + 1) * eb.shape[3]]
            if first and j == 0:
                continue
            dots = None
            for cs in chunks_of(channels):
                da = lax.dot_general(
                    e, w_ref[j, cs, :], (((1,), (1,)), ((), ())), preferred_element_type=jnp.float32
                )
                dv = da * gp[j, :, cs]
                dn = (
                    par_ref[j, 0:1, cs] * row_after(dv)
                    + par_ref[j, 1:2, cs] * dv
                    + par_ref[j, 2:3, cs] * row_before(dv)
                )
                m = dn * par_ref[j, 3:4, cs]
                mb[:, cs] = m
                part = jnp.sum(m * uh[j, :, cs], axis=-1, keepdims=True)
                dots = part if dots is None else dots + part
            mean = dots * (1.0 / channels)
            inv = inv_b[j, :, 0:1]
            dx = (gb[...] + inv * (mb[...] - uh[j] * mean)).astype(jnp.bfloat16)
            if last:
                gk_ref[j] = dx
        if not first:
            dx_ref[...] = dx


def backward_stage(stage, last, first, flags, g, weights, par, state, k, e):
    rows, channels = g.shape
    f32, bf = jnp.float32, jnp.bfloat16
    wide = (GROUP, rows, channels)
    args = [g, weights, par, *state]
    if first:
        args.append(k)
    args.append(e)
    args = [flags] + held(*args)
    out_shape = [kept(e.shape, bf)]
    if not first:
        out_shape.append(kept((rows, channels), bf))
    if last:
        out_shape.append(kept(wide, bf))
    return pl.pallas_call(
        functools.partial(backward_kernel, stage, last, first),
        out_shape=out_shape,
        in_specs=[SM] + [VM] * (len(args) - 1),
        out_specs=[VM] * len(out_shape),
        scratch_shapes=[pltpu.VMEM((rows, channels), f32)] * 2,
        input_output_aliases={len(args) - 1: 0},
        compiler_params=PARAMS,
        name=f"behind{stage}",
    )(*args)


def encode_bases(base_rows, embed_table):
    one_hot = (base_rows[:, :, None] == jnp.arange(4, dtype=jnp.int32)).astype(jnp.bfloat16)
    one_hot = one_hot.reshape(base_rows.shape[0], -1)
    return jnp.dot(one_hot, embed_table, preferred_element_type=jnp.float32).astype(jnp.bfloat16)


def swapped(block, distance):
    pairs = [(i, i ^ distance) for i in range(lax.axis_size(PIPE))]
    return lax.ppermute(block, PIPE, pairs)


def pack_kernel(places, flags, *rest):
    parts, out, sems = rest[: len(places)], rest[-2], rest[-1]
    copies = []
    for i, ((d, row), part) in enumerate(zip(places, parts)):
        slot = jnp.bitwise_xor(flags[1], d)
        target = out.at[slot, pl.ds(row, part.shape[0]), :]
        copies.append(pltpu.make_async_copy(part, target, sems.at[i]))
        copies[-1].start()
    for copy in copies:
        copy.wait()


def packed(stack, flags, items):
    places = [(d, row) for d, row, _ in items]
    parts = [part for _, _, part in items]
    channels = parts[0].shape[1]
    args, specs, aliases = [flags] + parts, [SM] + [ANY] * len(parts), {}
    if stack is not None:
        aliases = {len(args): 0}
        args += held(stack)
        specs.append(ANY)
    return pl.pallas_call(
        functools.partial(pack_kernel, places),
        out_shape=kept((GROUP, channels, channels), jnp.bfloat16),
        in_specs=specs,
        out_specs=ANY,
        scratch_shapes=[pltpu.SemaphoreType.DMA((len(parts),))],
        input_output_aliases=aliases,
        compiler_params=PARAMS,
        name="packed",
    )(*args)


def placed(stack, parts, member, row=0):
    for d, part in enumerate(parts):
        if part is not None:
            slot = jnp.bitwise_xor(member, d)
            stack = lax.dynamic_update_slice(stack, part[None], (slot, row, 0))
    return stack


def shifted(block, stage, to_stage):
    pairs = [(GROUP * stage + i, GROUP * to_stage + i) for i in range(MICROS)]
    return lax.ppermute(block, PIPE, pairs)


def traded(h):
    parts = [h[:1]]
    for d in range(1, GROUP):
        pairs = [(i, i ^ d) for i in range(lax.axis_size(PIPE)) if i % GROUP < MICROS]
        parts.append(lax.ppermute(h[d : d + 1], PIPE, pairs))
    return parts


def beside(group, count):
    if count == 1:
        return [group]
    return [group, lax.ppermute(group, "xl", [(i, i ^ 1) for i in range(count)])]


def term_kernel(places, errors, *rest):
    acts, out, ordered = rest[:-2], rest[-2], rest[-1]
    rows = errors.shape[1]
    total = None
    for shift, part in enumerate(acts):
        source = jnp.bitwise_xor(places[0], shift) * GROUP
        for d in range(GROUP):
            ordered[d * rows : (d + 1) * rows] = errors[source + jnp.bitwise_xor(places[1], d)]
        term = lax.dot_general(
            ordered[...],
            part[...].reshape(GROUP * rows, part.shape[2]),
            (((0,), (0,)), ((), ())),
            preferred_element_type=jnp.float32,
        )
        total = term if total is None else total + term
    out[...] = total.astype(out.dtype)


def gradient_block(places, errors, acts):
    args = held(errors, *acts)
    return pl.pallas_call(
        term_kernel,
        out_shape=kept((errors.shape[2], acts[0].shape[2]), jnp.bfloat16),
        in_specs=[SM] + [VM] * len(args),
        out_specs=VM,
        scratch_shapes=[pltpu.VMEM((GROUP * errors.shape[1], errors.shape[2]), jnp.bfloat16)],
        compiler_params=PARAMS,
        name="terms",
    )(places, *args)


def shards(base_ids, embed_table, segment_weights, conv_taps, norm_gains, cotangent):
    stages = lax.axis_size("g")
    pair, rest = lax.axis_size("xl"), lax.axis_size("xh") * lax.axis_size("y")
    member = lax.axis_index("q")
    flags = jnp.stack([lax.axis_index("g"), member]).astype(jnp.int32)
    micro = jnp.minimum(member, MICROS - 1)
    weight = segment_weights[0]
    channels = weight.shape[1]
    row_count = base_ids.shape[2]
    block = channels // pair
    bf = jnp.bfloat16

    across = swapped(weight, 2)
    x = encode_bases(base_ids[0, micro], embed_table)
    later, x = lax.optimization_barrier((weight, x))
    core_weight = swapped(later, 1)
    own = jnp.concatenate([conv_taps[0], norm_gains, jnp.zeros((4, channels), jnp.float32)])
    own, core_weight = lax.optimization_barrier((own, core_weight))
    par = placed(
        jnp.zeros((GROUP,) + own.shape, jnp.float32),
        [own] + [swapped(own, d) for d in range(1, GROUP)],
        member,
    )
    weights = packed(None, flags, [(0, 0, weight), (1, 0, core_weight)])
    across, weights, par, x = lax.optimization_barrier((across, weights, par, x))
    corner = swapped(across, 1)
    weights = packed(weights, flags, [(2, 0, across)])
    weights = packed(weights, flags, [(3, 0, corner)])
    h = jnp.zeros((GROUP, row_count, channels), bf)
    e = jnp.zeros((pair, GROUP, row_count, block), bf)
    states, k = [], None
    for stage in range(stages):
        skip, towers = stage == stages - 1, stage == 0
        outs = forward_stage(stage, skip, towers, flags, x, weights, par, k, h)
        states.append(outs[1:4])
        h = outs[4]
        if stage < stages - 1:
            x = shifted(outs[0], stage, stage + 1)
        if towers:
            x, tower = lax.optimization_barrier((x, outs[5]))
            k = shifted(tower, 0, stages - 1)

    g = cotangent[0, micro]
    returned = None
    for stage in reversed(range(stages)):
        last, first = stage == stages - 1, stage == 0
        outs = backward_stage(stage, last, first, flags, g, weights, par, states[stage], returned, e)
        e = outs[0]
        if stage > 0:
            g = shifted(outs[1], stage, stage - 1)
        if last:
            g, skip_grad = lax.optimization_barrier((g, outs[2]))
            returned = shifted(skip_grad, stages - 1, 0)
        if stage == stages - 2:
            h, e = lax.optimization_barrier((h, e))
            group = jnp.concatenate(traded(h))
        if stage == 1:
            group, e = lax.optimization_barrier((group, e))
    acts = beside(group, pair)
    errors = lax.all_to_all(e.reshape(-1, row_count, block), ("xl", "q"), 0, 0)
    places = jnp.stack([lax.axis_index("xl"), member]).astype(jnp.int32)
    turned = gradient_block(places, errors, acts)

    pieces = lax.all_to_all(turned.reshape(rest, block // rest, channels), ("xh", "y"), 0, 0)
    factor = 1.0 / math.sqrt(pair * rest * MICROS * row_count)
    piece = (jnp.sum(pieces.astype(jnp.float32), axis=0) * factor).astype(bf)
    piece = jnp.broadcast_to(piece, (pair * rest,) + piece.shape)
    whole = lax.all_to_all(piece, ("xl", "xh", "y"), 0, 0).reshape(channels, channels)
    return whole.T.astype(jnp.float32)[None]


def solution(mesh):
    replicas, _ = mesh.devices.shape
    low = math.gcd(2, replicas)
    high = math.gcd(2, replicas // low)
    shape = (replicas // (low * high), high, low, -1, GROUP)
    grid = Mesh(mesh.devices.reshape(shape), ("y", "xh", "xl", "g", "q"))
    windows = P(("y", "xh", "xl"), None, None, None)
    return jax.shard_map(
        shards,
        mesh=grid,
        in_specs=(
            windows,
            P(),
            P(PIPE, None, None),
            P(PIPE, None, None),
            P(PIPE, None),
            windows,
        ),
        out_specs=P(PIPE, None, None),
        check_vma=False,
    )
```

```python
import functools
import math

import jax
import jax.numpy as jnp
from jax import lax
from jax.experimental import pallas as pl
from jax.experimental.pallas import tpu as pltpu
from jax.sharding import Mesh
from jax.sharding import PartitionSpec as P

GROUP = 4
MICROS = 3
CHUNK = 256
PIPE = ("g", "q")
ANY = pl.BlockSpec(memory_space=pl.ANY)
VM = pl.BlockSpec(memory_space=pltpu.VMEM)
SM = pl.BlockSpec(memory_space=pltpu.SMEM)
PARAMS = pltpu.CompilerParams(vmem_limit_bytes=4 * 1024 * 1024)
CUBIC = 0.044715
SCALE = math.sqrt(2.0 / math.pi)


def row_before(block):
    rows = lax.broadcasted_iota(jnp.int32, block.shape, 0)
    return jnp.where(rows == 0, 0.0, pltpu.roll(block, 1, 0))


def row_after(block):
    size = block.shape[0]
    rows = lax.broadcasted_iota(jnp.int32, block.shape, 0)
    return jnp.where(rows == size - 1, 0.0, pltpu.roll(block, size - 1, 0))


def chunks_of(channels):
    return [slice(c, c + CHUNK) for c in range(0, channels, CHUNK)]


def forward_kernel(stage, skip, towers, flags, x_ref, w_ref, par_ref, *rest):
    rest = list(rest)
    k_ref = rest.pop(0) if skip else None
    h_ref = rest.pop(0)
    y_ref, uh, gp, inv_b, hb = rest[:5]
    rest = rest[5:]
    ys = rest.pop(0) if towers else None
    (ub,) = rest
    channels = x_ref.shape[1]
    member = flags[1]
    active = (flags[0] == stage) & (member < MICROS)

    @pl.when(jnp.logical_not(active))
    def _():
        hb[...] = h_ref[...]

    @pl.when(active)
    def _():
        y = x_ref[...]
        for j in range(GROUP):
            d = jnp.bitwise_xor(member, j)
            squares = None
            for cs in chunks_of(channels):
                u = y[:, cs].astype(jnp.float32)
                if skip:
                    u = u + k_ref[j, :, cs].astype(jnp.float32)
                ub[:, cs] = u
                part = jnp.sum(u * u, axis=-1, keepdims=True)
                squares = part if squares is None else squares + part
            inv = lax.rsqrt(squares * (1.0 / channels) + 1e-06)
            inv_b[j] = jnp.broadcast_to(inv, inv_b.shape[1:])
            total = None
            for cs in chunks_of(channels):
                unit = ub[:, cs] * inv
                uh[j, :, cs] = unit
                n = unit * par_ref[j, 3:4, cs]
                v = (
                    par_ref[j, 0:1, cs] * row_before(n)
                    + par_ref[j, 1:2, cs] * n
                    + par_ref[j, 2:3, cs] * row_after(n)
                )
                v2 = v * v
                th = jnp.tanh(v * (SCALE + (SCALE * CUBIC) * v2))
                half = 0.5 * (1.0 + th)
                gp[j, :, cs] = half + (0.5 * v) * (1.0 - th * th) * (
                    SCALE + (3.0 * SCALE * CUBIC) * v2
                )
                act = (v * half).astype(jnp.bfloat16)
                hb[d, :, cs] = act
                part = jnp.dot(act, w_ref[j, cs, :], preferred_element_type=jnp.float32)
                total = part if total is None else total + part
            y = (ub[...] + total).astype(jnp.bfloat16)
            if towers:
                ys[j] = y
        y_ref[...] = y


def kept(shape, kind):
    return pltpu.VMEM(shape, kind)


def held(*arrays):
    return [pltpu.with_memory_space_constraint(a, pltpu.VMEM) for a in arrays]


def forward_stage(stage, skip, towers, flags, x, weights, par, k, h):
    rows, channels = x.shape
    f32, bf = jnp.float32, jnp.bfloat16
    wide = (GROUP, rows, channels)
    thin = (GROUP, rows, 128)
    out_shape = [
        kept((rows, channels), bf),
        kept(wide, f32),
        kept(wide, f32),
        kept(thin, f32),
        kept(wide, bf),
    ]
    if towers:
        out_shape.append(kept(wide, bf))
    args = [x, weights, par]
    if skip:
        args.append(k)
    args.append(h)
    args = [flags] + held(*args)
    return pl.pallas_call(
        functools.partial(forward_kernel, stage, skip, towers),
        out_shape=out_shape,
        in_specs=[SM] + [VM] * (len(args) - 1),
        out_specs=[VM] * len(out_shape),
        scratch_shapes=[pltpu.VMEM((rows, channels), f32)],
        input_output_aliases={len(args) - 1: 4},
        compiler_params=PARAMS,
        name=f"ahead{stage}",
    )(*args)


def backward_kernel(stage, last, first, flags, g_ref, w_ref, par_ref, uh, gp, inv_b, *rest):
    rest = list(rest)
    k_ref = rest.pop(0) if first else None
    e_ref = rest.pop(0)
    eb = rest.pop(0)
    dx_ref = None if first else rest.pop(0)
    gk_ref = rest.pop(0) if last else None
    gb, mb = rest
    channels = g_ref.shape[1]
    member = flags[1]
    active = (flags[0] == stage) & (member < MICROS)

    @pl.when(jnp.logical_not(active))
    def _():
        eb[...] = e_ref[...]

    @pl.when(active)
    def _():
        dx = g_ref[...]
        for j in reversed(range(GROUP)):
            d = jnp.bitwise_xor(member, j)
            for cs in chunks_of(channels):
                g = dx[:, cs].astype(jnp.float32)
                if first:
                    g = g + k_ref[j, :, cs].astype(jnp.float32)
                gb[:, cs] = g
            e = gb[...].astype(jnp.bfloat16)
            eb[d] = e
            if first and j == 0:
                continue
            dots = None
            for cs in chunks_of(channels):
                da = lax.dot_general(
                    e, w_ref[j, cs, :], (((1,), (1,)), ((), ())), preferred_element_type=jnp.float32
                )
                dv = da * gp[j, :, cs]
                dn = (
                    par_ref[j, 0:1, cs] * row_after(dv)
                    + par_ref[j, 1:2, cs] * dv
                    + par_ref[j, 2:3, cs] * row_before(dv)
                )
                m = dn * par_ref[j, 3:4, cs]
                mb[:, cs] = m
                part = jnp.sum(m * uh[j, :, cs], axis=-1, keepdims=True)
                dots = part if dots is None else dots + part
            mean = dots * (1.0 / channels)
            inv = inv_b[j, :, 0:1]
            dx = (gb[...] + inv * (mb[...] - uh[j] * mean)).astype(jnp.bfloat16)
            if last:
                gk_ref[j] = dx
        if not first:
            dx_ref[...] = dx


def backward_stage(stage, last, first, flags, g, weights, par, state, k, e):
    rows, channels = g.shape
    f32, bf = jnp.float32, jnp.bfloat16
    wide = (GROUP, rows, channels)
    args = [g, weights, par, *state]
    if first:
        args.append(k)
    args.append(e)
    args = [flags] + held(*args)
    out_shape = [kept(wide, bf)]
    if not first:
        out_shape.append(kept((rows, channels), bf))
    if last:
        out_shape.append(kept(wide, bf))
    return pl.pallas_call(
        functools.partial(backward_kernel, stage, last, first),
        out_shape=out_shape,
        in_specs=[SM] + [VM] * (len(args) - 1),
        out_specs=[VM] * len(out_shape),
        scratch_shapes=[pltpu.VMEM((rows, channels), f32)] * 2,
        input_output_aliases={len(args) - 1: 0},
        compiler_params=PARAMS,
        name=f"behind{stage}",
    )(*args)


def encode_bases(base_rows, embed_table):
    one_hot = (base_rows[:, :, None] == jnp.arange(4, dtype=jnp.int32)).astype(jnp.bfloat16)
    one_hot = one_hot.reshape(base_rows.shape[0], -1)
    return jnp.dot(one_hot, embed_table, preferred_element_type=jnp.float32).astype(jnp.bfloat16)


def swapped(block, distance):
    pairs = [(i, i ^ distance) for i in range(lax.axis_size(PIPE))]
    return lax.ppermute(block, PIPE, pairs)


def pack_kernel(places, flags, *rest):
    parts, out, sems = rest[: len(places)], rest[-2], rest[-1]
    copies = []
    for i, ((d, row), part) in enumerate(zip(places, parts)):
        slot = jnp.bitwise_xor(flags[1], d)
        target = out.at[slot, pl.ds(row, part.shape[0]), :]
        copies.append(pltpu.make_async_copy(part, target, sems.at[i]))
        copies[-1].start()
    for copy in copies:
        copy.wait()


def packed(stack, flags, items):
    places = [(d, row) for d, row, _ in items]
    parts = [part for _, _, part in items]
    channels = parts[0].shape[1]
    args, specs, aliases = [flags] + parts, [SM] + [ANY] * len(parts), {}
    if stack is not None:
        aliases = {len(args): 0}
        args += held(stack)
        specs.append(ANY)
    return pl.pallas_call(
        functools.partial(pack_kernel, places),
        out_shape=kept((GROUP, channels, channels), jnp.bfloat16),
        in_specs=specs,
        out_specs=ANY,
        scratch_shapes=[pltpu.SemaphoreType.DMA((len(parts),))],
        input_output_aliases=aliases,
        compiler_params=PARAMS,
        name="packed",
    )(*args)


def placed(stack, parts, member, row=0):
    for d, part in enumerate(parts):
        if part is not None:
            slot = jnp.bitwise_xor(member, d)
            stack = lax.dynamic_update_slice(stack, part[None], (slot, row, 0))
    return stack


def shifted(block, stage, to_stage):
    pairs = [(GROUP * stage + i, GROUP * to_stage + i) for i in range(MICROS)]
    return lax.ppermute(block, PIPE, pairs)


def traded(block, distance):
    pairs = [(i, i ^ distance) for i in range(lax.axis_size(PIPE)) if i % GROUP < MICROS]
    return lax.ppermute(block[distance], PIPE, pairs)


def together(block):
    return jnp.concatenate([block[0]] + [traded(block, d) for d in range(1, GROUP)])


def summed_part(block, axis):
    count = lax.axis_size(axis)
    parts = lax.all_to_all(block.reshape(count, -1, block.shape[1]), axis, 0, 0)
    return jnp.sum(parts.astype(jnp.float32), axis=0)


def all_parts(block, axis):
    count = lax.axis_size(axis)
    parts = lax.all_to_all(jnp.broadcast_to(block, (count,) + block.shape), axis, 0, 0)
    return parts.reshape(-1, block.shape[1])


def shards(base_ids, embed_table, segment_weights, conv_taps, norm_gains, cotangent):
    stages = lax.axis_size("g")
    member = lax.axis_index("q")
    flags = jnp.stack([lax.axis_index("g"), member]).astype(jnp.int32)
    micro = jnp.minimum(member, MICROS - 1)
    weight = segment_weights[0]
    channels = weight.shape[1]
    row_count = base_ids.shape[2]
    bf = jnp.bfloat16

    across = swapped(weight, 2)
    x = encode_bases(base_ids[0, micro], embed_table)
    later, x = lax.optimization_barrier((weight, x))
    beside = swapped(later, 1)
    own = jnp.concatenate([conv_taps[0], norm_gains, jnp.zeros((4, channels), jnp.float32)])
    own, beside = lax.optimization_barrier((own, beside))
    par = placed(
        jnp.zeros((GROUP,) + own.shape, jnp.float32),
        [own] + [swapped(own, d) for d in range(1, GROUP)],
        member,
    )
    weights = packed(None, flags, [(0, 0, weight), (1, 0, beside)])
    across, weights, par, x = lax.optimization_barrier((across, weights, par, x))
    corner = swapped(across, 1)
    weights = packed(weights, flags, [(2, 0, across)])
    weights = packed(weights, flags, [(3, 0, corner)])

    wide = (GROUP, row_count, channels)
    h = jnp.zeros(wide, bf)
    e = jnp.zeros(wide, bf)
    states, k = [], None
    for stage in range(stages):
        skip, towers = stage == stages - 1, stage == 0
        outs = forward_stage(stage, skip, towers, flags, x, weights, par, k, h)
        states.append(outs[1:4])
        h = outs[4]
        if stage < stages - 1:
            x = shifted(outs[0], stage, stage + 1)
        if towers:
            x, tower = lax.optimization_barrier((x, outs[5]))
            k = shifted(tower, 0, stages - 1)

    g = cotangent[0, micro]
    returned = None
    for stage in reversed(range(stages)):
        last, first = stage == stages - 1, stage == 0
        outs = backward_stage(stage, last, first, flags, g, weights, par, states[stage], returned, e)
        e = outs[0]
        if stage > 0:
            g = shifted(outs[1], stage, stage - 1)
        if last:
            g, skip_grad = lax.optimization_barrier((g, outs[2]))
            returned = shifted(skip_grad, stages - 1, 0)
        if stage == stages - 2:
            h, e = lax.optimization_barrier((h, e))
            acts = together(h)
    errors = together(e)

    terms = lax.dot_general(acts, errors, (((0,), (0,)), ((), ())), preferred_element_type=jnp.float32)
    factor = 1.0 / math.sqrt(lax.axis_size(("y", "x")) * MICROS * row_count)
    part = summed_part(terms.astype(bf), "x").astype(bf)
    part = (summed_part(part, "y") * factor).astype(bf)
    whole = all_parts(all_parts(part, "y"), "x")
    return whole.astype(jnp.float32)[None]


def solution(mesh):
    replicas, _ = mesh.devices.shape
    wide = math.gcd(4, replicas)
    grid = Mesh(mesh.devices.reshape(replicas // wide, wide, -1, GROUP), ("y", "x", "g", "q"))
    windows = P(("y", "x"), None, None, None)
    return jax.shard_map(
        shards,
        mesh=grid,
        in_specs=(
            windows,
            P(),
            P(PIPE, None, None),
            P(PIPE, None, None),
            P(PIPE, None),
            windows,
        ),
        out_specs=P(PIPE, None, None),
        check_vma=False,
    )
```

```python
import functools
import math

import jax
import jax.numpy as jnp
from jax import lax
from jax.experimental import pallas as pl
from jax.experimental.pallas import tpu as pltpu
from jax.sharding import Mesh
from jax.sharding import PartitionSpec as P

GROUP = 4
MICROS = 3
CHUNK = 384
PIPE = ("g", "q")
ANY = pl.BlockSpec(memory_space=pl.ANY)
VM = pl.BlockSpec(memory_space=pltpu.VMEM)
SM = pl.BlockSpec(memory_space=pltpu.SMEM)
PARAMS = pltpu.CompilerParams(vmem_limit_bytes=4 * 1024 * 1024)
CUBIC = 0.044715
SCALE = math.sqrt(2.0 / math.pi)


def row_before(block):
    rows = lax.broadcasted_iota(jnp.int32, block.shape, 0)
    return jnp.where(rows == 0, 0.0, pltpu.roll(block, 1, 0))


def row_after(block):
    size = block.shape[0]
    rows = lax.broadcasted_iota(jnp.int32, block.shape, 0)
    return jnp.where(rows == size - 1, 0.0, pltpu.roll(block, size - 1, 0))


def chunks_of(channels):
    return [slice(c, c + CHUNK) for c in range(0, channels, CHUNK)]


def forward_kernel(stage, skip, towers, flags, x_ref, w_ref, par_ref, *rest):
    rest = list(rest)
    k_ref = rest.pop(0) if skip else None
    h_ref = rest.pop(0)
    y_ref, uh, gp, inv_b, hb = rest[:5]
    rest = rest[5:]
    ys = rest.pop(0) if towers else None
    (ub,) = rest
    channels = x_ref.shape[1]
    member = flags[1]
    active = (flags[0] == stage) & (member < MICROS)

    @pl.when(jnp.logical_not(active))
    def _():
        hb[...] = h_ref[...]

    @pl.when(active)
    def _():
        y = x_ref[...]
        for j in range(GROUP):
            d = jnp.bitwise_xor(member, j)
            squares = None
            for cs in chunks_of(channels):
                u = y[:, cs].astype(jnp.float32)
                if skip:
                    u = u + k_ref[j, :, cs].astype(jnp.float32)
                ub[:, cs] = u
                part = jnp.sum(u * u, axis=-1, keepdims=True)
                squares = part if squares is None else squares + part
            inv = lax.rsqrt(squares * (1.0 / channels) + 1e-06)
            inv_b[j] = jnp.broadcast_to(inv, inv_b.shape[1:])
            total = None
            for cs in chunks_of(channels):
                unit = ub[:, cs] * inv
                uh[j, :, cs] = unit
                n = unit * par_ref[j, 3:4, cs]
                v = (
                    par_ref[j, 0:1, cs] * row_before(n)
                    + par_ref[j, 1:2, cs] * n
                    + par_ref[j, 2:3, cs] * row_after(n)
                )
                v2 = v * v
                th = jnp.tanh(v * (SCALE + (SCALE * CUBIC) * v2))
                half = 0.5 * (1.0 + th)
                gp[j, :, cs] = half + (0.5 * v) * (1.0 - th * th) * (
                    SCALE + (3.0 * SCALE * CUBIC) * v2
                )
                act = (v * half).astype(jnp.bfloat16)
                hb[d, :, cs] = act
                part = jnp.dot(act, w_ref[j, cs, :], preferred_element_type=jnp.float32)
                total = part if total is None else total + part
            y = (ub[...] + total).astype(jnp.bfloat16)
            if towers:
                ys[j] = y
        y_ref[...] = y


def kept(shape, kind):
    return pltpu.VMEM(shape, kind)


def held(*arrays):
    return [pltpu.with_memory_space_constraint(a, pltpu.VMEM) for a in arrays]


def forward_stage(stage, skip, towers, flags, x, weights, par, k, h):
    rows, channels = x.shape
    f32, bf = jnp.float32, jnp.bfloat16
    wide = (GROUP, rows, channels)
    thin = (GROUP, rows, 128)
    out_shape = [
        kept((rows, channels), bf),
        kept(wide, f32),
        kept(wide, f32),
        kept(thin, f32),
        kept(wide, bf),
    ]
    if towers:
        out_shape.append(kept(wide, bf))
    args = [x, weights, par]
    if skip:
        args.append(k)
    args.append(h)
    args = [flags] + held(*args)
    return pl.pallas_call(
        functools.partial(forward_kernel, stage, skip, towers),
        out_shape=out_shape,
        in_specs=[SM] + [VM] * (len(args) - 1),
        out_specs=[VM] * len(out_shape),
        scratch_shapes=[pltpu.VMEM((rows, channels), f32)],
        input_output_aliases={len(args) - 1: 4},
        compiler_params=PARAMS,
        name=f"ahead{stage}",
    )(*args)


def backward_kernel(stage, last, first, flags, g_ref, w_ref, par_ref, uh, gp, inv_b, *rest):
    rest = list(rest)
    k_ref = rest.pop(0) if first else None
    e_ref = rest.pop(0)
    eb = rest.pop(0)
    dx_ref = None if first else rest.pop(0)
    gk_ref = rest.pop(0) if last else None
    gb, mb = rest
    channels = g_ref.shape[1]
    member = flags[1]
    active = (flags[0] == stage) & (member < MICROS)

    @pl.when(jnp.logical_not(active))
    def _():
        eb[...] = e_ref[...]

    @pl.when(active)
    def _():
        dx = g_ref[...]
        for j in reversed(range(GROUP)):
            d = jnp.bitwise_xor(member, j)
            for cs in chunks_of(channels):
                g = dx[:, cs].astype(jnp.float32)
                if first:
                    g = g + k_ref[j, :, cs].astype(jnp.float32)
                gb[:, cs] = g
            e = gb[...].astype(jnp.bfloat16)
            eb[d] = e
            if first and j == 0:
                continue
            dots = None
            for cs in chunks_of(channels):
                da = lax.dot_general(
                    e, w_ref[j, cs, :], (((1,), (1,)), ((), ())), preferred_element_type=jnp.float32
                )
                dv = da * gp[j, :, cs]
                dn = (
                    par_ref[j, 0:1, cs] * row_after(dv)
                    + par_ref[j, 1:2, cs] * dv
                    + par_ref[j, 2:3, cs] * row_before(dv)
                )
                m = dn * par_ref[j, 3:4, cs]
                mb[:, cs] = m
                part = jnp.sum(m * uh[j, :, cs], axis=-1, keepdims=True)
                dots = part if dots is None else dots + part
            mean = dots * (1.0 / channels)
            inv = inv_b[j, :, 0:1]
            dx = (gb[...] + inv * (mb[...] - uh[j] * mean)).astype(jnp.bfloat16)
            if last:
                gk_ref[j] = dx
        if not first:
            dx_ref[...] = dx


def backward_stage(stage, last, first, flags, g, weights, par, state, k, e):
    rows, channels = g.shape
    f32, bf = jnp.float32, jnp.bfloat16
    wide = (GROUP, rows, channels)
    args = [g, weights, par, *state]
    if first:
        args.append(k)
    args.append(e)
    args = [flags] + held(*args)
    out_shape = [kept(wide, bf)]
    if not first:
        out_shape.append(kept((rows, channels), bf))
    if last:
        out_shape.append(kept(wide, bf))
    return pl.pallas_call(
        functools.partial(backward_kernel, stage, last, first),
        out_shape=out_shape,
        in_specs=[SM] + [VM] * (len(args) - 1),
        out_specs=[VM] * len(out_shape),
        scratch_shapes=[pltpu.VMEM((rows, channels), f32)] * 2,
        input_output_aliases={len(args) - 1: 0},
        compiler_params=PARAMS,
        name=f"behind{stage}",
    )(*args)


def encode_bases(base_rows, embed_table):
    one_hot = (base_rows[:, :, None] == jnp.arange(4, dtype=jnp.int32)).astype(jnp.bfloat16)
    one_hot = one_hot.reshape(base_rows.shape[0], -1)
    return jnp.dot(one_hot, embed_table, preferred_element_type=jnp.float32).astype(jnp.bfloat16)


def swapped(block, distance):
    pairs = [(i, i ^ distance) for i in range(lax.axis_size(PIPE))]
    return lax.ppermute(block, PIPE, pairs)


def pack_kernel(places, flags, *rest):
    parts, out, sems = rest[: len(places)], rest[-2], rest[-1]
    copies = []
    for i, ((d, row), part) in enumerate(zip(places, parts)):
        slot = jnp.bitwise_xor(flags[1], d)
        target = out.at[slot, pl.ds(row, part.shape[0]), :]
        copies.append(pltpu.make_async_copy(part, target, sems.at[i]))
        copies[-1].start()
    for copy in copies:
        copy.wait()


def packed(stack, flags, items):
    places = [(d, row) for d, row, _ in items]
    parts = [part for _, _, part in items]
    channels = parts[0].shape[1]
    args, specs, aliases = [flags] + parts, [SM] + [ANY] * len(parts), {}
    if stack is not None:
        aliases = {len(args): 0}
        args += held(stack)
        specs.append(ANY)
    return pl.pallas_call(
        functools.partial(pack_kernel, places),
        out_shape=kept((GROUP, channels, channels), jnp.bfloat16),
        in_specs=specs,
        out_specs=ANY,
        scratch_shapes=[pltpu.SemaphoreType.DMA((len(parts),))],
        input_output_aliases=aliases,
        compiler_params=PARAMS,
        name="packed",
    )(*args)


def placed(stack, parts, member, row=0):
    for d, part in enumerate(parts):
        if part is not None:
            slot = jnp.bitwise_xor(member, d)
            stack = lax.dynamic_update_slice(stack, part[None], (slot, row, 0))
    return stack


def shifted(block, stage, to_stage):
    pairs = [(GROUP * stage + i, GROUP * to_stage + i) for i in range(MICROS)]
    return lax.ppermute(block, PIPE, pairs)


def traded(block, distance):
    pairs = [(i, i ^ distance) for i in range(lax.axis_size(PIPE)) if i % GROUP < MICROS]
    return lax.ppermute(block[distance], PIPE, pairs)


def together(block):
    return jnp.concatenate([block[0]] + [traded(block, d) for d in range(1, GROUP)])


def summed_part(block, axis):
    count = lax.axis_size(axis)
    parts = lax.all_to_all(block.reshape(count, -1, block.shape[1]), axis, 0, 0)
    return jnp.sum(parts.astype(jnp.float32), axis=0)


def all_parts(block, axis):
    count = lax.axis_size(axis)
    parts = lax.all_to_all(jnp.broadcast_to(block, (count,) + block.shape), axis, 0, 0)
    return parts.reshape(-1, block.shape[1])


def shards(base_ids, embed_table, segment_weights, conv_taps, norm_gains, cotangent):
    stages = lax.axis_size("g")
    member = lax.axis_index("q")
    flags = jnp.stack([lax.axis_index("g"), member]).astype(jnp.int32)
    micro = jnp.minimum(member, MICROS - 1)
    weight = segment_weights[0]
    channels = weight.shape[1]
    row_count = base_ids.shape[2]
    bf = jnp.bfloat16

    across = swapped(weight, 2)
    beside = swapped(weight, 1)
    own = jnp.concatenate([conv_taps[0], norm_gains, jnp.zeros((4, channels), jnp.float32)])
    own, base_ids, beside = lax.optimization_barrier((own, base_ids, beside))
    x = encode_bases(base_ids[0, micro], embed_table)
    par = placed(
        jnp.zeros((GROUP,) + own.shape, jnp.float32),
        [own] + [swapped(own, d) for d in range(1, GROUP)],
        member,
    )
    weights = packed(None, flags, [(0, 0, weight), (1, 0, beside)])
    across, weights, par, x = lax.optimization_barrier((across, weights, par, x))
    corner = swapped(across, 1)
    weights = packed(weights, flags, [(2, 0, across)])
    weights = packed(weights, flags, [(3, 0, corner)])

    wide = (GROUP, row_count, channels)
    h = jnp.zeros(wide, bf)
    e = jnp.zeros(wide, bf)
    states, k = [], None
    for stage in range(stages):
        skip, towers = stage == stages - 1, stage == 0
        outs = forward_stage(stage, skip, towers, flags, x, weights, par, k, h)
        states.append(outs[1:4])
        h = outs[4]
        if stage < stages - 1:
            x = shifted(outs[0], stage, stage + 1)
        if towers:
            x, tower = lax.optimization_barrier((x, outs[5]))
            k = shifted(tower, 0, stages - 1)

    g = cotangent[0, micro]
    returned = None
    for stage in reversed(range(stages)):
        last, first = stage == stages - 1, stage == 0
        outs = backward_stage(stage, last, first, flags, g, weights, par, states[stage], returned, e)
        e = outs[0]
        if stage > 0:
            g = shifted(outs[1], stage, stage - 1)
        if last:
            g, skip_grad = lax.optimization_barrier((g, outs[2]))
            returned = shifted(skip_grad, stages - 1, 0)
        if stage == stages - 2:
            h, e = lax.optimization_barrier((h, e))
            acts = together(h)
        if stage == 1:
            acts, e = lax.optimization_barrier((acts, e))
    errors = together(e)

    terms = lax.dot_general(acts, errors, (((0,), (0,)), ((), ())), preferred_element_type=jnp.float32)
    factor = 1.0 / math.sqrt(lax.axis_size(("y", "x")) * MICROS * row_count)
    part = summed_part(terms.astype(bf), "x").astype(bf)
    part = (summed_part(part, "y") * factor).astype(bf)
    whole = all_parts(all_parts(part, "y"), "x")
    return whole.astype(jnp.float32)[None]


def solution(mesh):
    replicas, _ = mesh.devices.shape
    wide = math.gcd(4, replicas)
    grid = Mesh(mesh.devices.reshape(replicas // wide, wide, -1, GROUP), ("y", "x", "g", "q"))
    windows = P(("y", "x"), None, None, None)
    return jax.shard_map(
        shards,
        mesh=grid,
        in_specs=(
            windows,
            P(),
            P(PIPE, None, None),
            P(PIPE, None, None),
            P(PIPE, None),
            windows,
        ),
        out_specs=P(PIPE, None, None),
        check_vma=False,
    )
```

```python
import functools
import math

import jax
import jax.numpy as jnp
from jax import lax
from jax.experimental import pallas as pl
from jax.experimental.pallas import tpu as pltpu
from jax.sharding import Mesh
from jax.sharding import PartitionSpec as P

GROUP = 4
MICROS = 3
CHUNK = 384
PIPE = ("g", "q")
NEAR = ("yl", "x")
ANY = pl.BlockSpec(memory_space=pl.ANY)
VM = pl.BlockSpec(memory_space=pltpu.VMEM)
SM = pl.BlockSpec(memory_space=pltpu.SMEM)
PARAMS = pltpu.CompilerParams(vmem_limit_bytes=4 * 1024 * 1024)
CUBIC = 0.044715
SCALE = math.sqrt(2.0 / math.pi)


def row_before(block):
    rows = lax.broadcasted_iota(jnp.int32, block.shape, 0)
    return jnp.where(rows == 0, 0.0, pltpu.roll(block, 1, 0))


def row_after(block):
    size = block.shape[0]
    rows = lax.broadcasted_iota(jnp.int32, block.shape, 0)
    return jnp.where(rows == size - 1, 0.0, pltpu.roll(block, size - 1, 0))


def chunks_of(channels):
    return [slice(c, c + CHUNK) for c in range(0, channels, CHUNK)]


def forward_kernel(stage, skip, towers, flags, x_ref, w_ref, par_ref, *rest):
    rest = list(rest)
    k_ref = rest.pop(0) if skip else None
    h_ref = rest.pop(0)
    y_ref, uh, gp, inv_b, hb = rest[:5]
    rest = rest[5:]
    ys = rest.pop(0) if towers else None
    (ub,) = rest
    channels = x_ref.shape[1]
    member = flags[1]
    active = (flags[0] == stage) & (member < MICROS)

    @pl.when(jnp.logical_not(active))
    def _():
        hb[...] = h_ref[...]

    @pl.when(active)
    def _():
        y = x_ref[...]
        for j in range(GROUP):
            d = jnp.bitwise_xor(member, j)
            squares = None
            for cs in chunks_of(channels):
                u = y[:, cs].astype(jnp.float32)
                if skip:
                    u = u + k_ref[j, :, cs].astype(jnp.float32)
                ub[:, cs] = u
                part = jnp.sum(u * u, axis=-1, keepdims=True)
                squares = part if squares is None else squares + part
            inv = lax.rsqrt(squares * (1.0 / channels) + 1e-06)
            inv_b[j] = jnp.broadcast_to(inv, inv_b.shape[1:])
            total = None
            for cs in chunks_of(channels):
                unit = ub[:, cs] * inv
                uh[j, :, cs] = unit
                n = unit * par_ref[j, 3:4, cs]
                v = (
                    par_ref[j, 0:1, cs] * row_before(n)
                    + par_ref[j, 1:2, cs] * n
                    + par_ref[j, 2:3, cs] * row_after(n)
                )
                v2 = v * v
                th = jnp.tanh(v * (SCALE + (SCALE * CUBIC) * v2))
                half = 0.5 * (1.0 + th)
                gp[j, :, cs] = half + (0.5 * v) * (1.0 - th * th) * (
                    SCALE + (3.0 * SCALE * CUBIC) * v2
                )
                act = (v * half).astype(jnp.bfloat16)
                hb[d, :, cs] = act
                part = jnp.dot(act, w_ref[j, cs, :], preferred_element_type=jnp.float32)
                total = part if total is None else total + part
            y = (ub[...] + total).astype(jnp.bfloat16)
            if towers:
                ys[j] = y
        y_ref[...] = y


def kept(shape, kind):
    return pltpu.VMEM(shape, kind)


def held(*arrays):
    return [pltpu.with_memory_space_constraint(a, pltpu.VMEM) for a in arrays]


def forward_stage(stage, skip, towers, flags, x, weights, par, k, h):
    rows, channels = x.shape
    f32, bf = jnp.float32, jnp.bfloat16
    wide = (GROUP, rows, channels)
    thin = (GROUP, rows, 128)
    out_shape = [
        kept((rows, channels), bf),
        kept(wide, f32),
        kept(wide, f32),
        kept(thin, f32),
        kept(wide, bf),
    ]
    if towers:
        out_shape.append(kept(wide, bf))
    args = [x, weights, par]
    if skip:
        args.append(k)
    args.append(h)
    args = [flags] + held(*args)
    return pl.pallas_call(
        functools.partial(forward_kernel, stage, skip, towers),
        out_shape=out_shape,
        in_specs=[SM] + [VM] * (len(args) - 1),
        out_specs=[VM] * len(out_shape),
        scratch_shapes=[pltpu.VMEM((rows, channels), f32)],
        input_output_aliases={len(args) - 1: 4},
        compiler_params=PARAMS,
        name=f"ahead{stage}",
    )(*args)


def backward_kernel(stage, last, first, flags, g_ref, w_ref, par_ref, uh, gp, inv_b, *rest):
    rest = list(rest)
    k_ref = rest.pop(0) if first else None
    e_ref = rest.pop(0)
    eb = rest.pop(0)
    dx_ref = None if first else rest.pop(0)
    gk_ref = rest.pop(0) if last else None
    gb, mb = rest
    channels = g_ref.shape[1]
    member = flags[1]
    active = (flags[0] == stage) & (member < MICROS)

    @pl.when(jnp.logical_not(active))
    def _():
        eb[...] = e_ref[...]

    @pl.when(active)
    def _():
        dx = g_ref[...]
        for j in reversed(range(GROUP)):
            d = jnp.bitwise_xor(member, j)
            for cs in chunks_of(channels):
                g = dx[:, cs].astype(jnp.float32)
                if first:
                    g = g + k_ref[j, :, cs].astype(jnp.float32)
                gb[:, cs] = g
            e = gb[...].astype(jnp.bfloat16)
            eb[d] = e
            if first and j == 0:
                continue
            dots = None
            for cs in chunks_of(channels):
                da = lax.dot_general(
                    e, w_ref[j, cs, :], (((1,), (1,)), ((), ())), preferred_element_type=jnp.float32
                )
                dv = da * gp[j, :, cs]
                dn = (
                    par_ref[j, 0:1, cs] * row_after(dv)
                    + par_ref[j, 1:2, cs] * dv
                    + par_ref[j, 2:3, cs] * row_before(dv)
                )
                m = dn * par_ref[j, 3:4, cs]
                mb[:, cs] = m
                part = jnp.sum(m * uh[j, :, cs], axis=-1, keepdims=True)
                dots = part if dots is None else dots + part
            mean = dots * (1.0 / channels)
            inv = inv_b[j, :, 0:1]
            dx = (gb[...] + inv * (mb[...] - uh[j] * mean)).astype(jnp.bfloat16)
            if last:
                gk_ref[j] = dx
        if not first:
            dx_ref[...] = dx


def backward_stage(stage, last, first, flags, g, weights, par, state, k, e):
    rows, channels = g.shape
    f32, bf = jnp.float32, jnp.bfloat16
    wide = (GROUP, rows, channels)
    args = [g, weights, par, *state]
    if first:
        args.append(k)
    args.append(e)
    args = [flags] + held(*args)
    out_shape = [kept(wide, bf)]
    if not first:
        out_shape.append(kept((rows, channels), bf))
    if last:
        out_shape.append(kept(wide, bf))
    return pl.pallas_call(
        functools.partial(backward_kernel, stage, last, first),
        out_shape=out_shape,
        in_specs=[SM] + [VM] * (len(args) - 1),
        out_specs=[VM] * len(out_shape),
        scratch_shapes=[pltpu.VMEM((rows, channels), f32)] * 2,
        input_output_aliases={len(args) - 1: 0},
        compiler_params=PARAMS,
        name=f"behind{stage}",
    )(*args)


def encode_bases(base_rows, embed_table):
    one_hot = (base_rows[:, :, None] == jnp.arange(4, dtype=jnp.int32)).astype(jnp.bfloat16)
    one_hot = one_hot.reshape(base_rows.shape[0], -1)
    return jnp.dot(one_hot, embed_table, preferred_element_type=jnp.float32).astype(jnp.bfloat16)


def swapped(block, distance):
    pairs = [(i, i ^ distance) for i in range(lax.axis_size(PIPE))]
    return lax.ppermute(block, PIPE, pairs)


def pack_kernel(places, flags, *rest):
    parts, out, sems = rest[: len(places)], rest[-2], rest[-1]
    copies = []
    for i, ((d, row), part) in enumerate(zip(places, parts)):
        slot = jnp.bitwise_xor(flags[1], d)
        target = out.at[slot, pl.ds(row, part.shape[0]), :]
        copies.append(pltpu.make_async_copy(part, target, sems.at[i]))
        copies[-1].start()
    for copy in copies:
        copy.wait()


def packed(stack, flags, items):
    places = [(d, row) for d, row, _ in items]
    parts = [part for _, _, part in items]
    channels = parts[0].shape[1]
    args, specs, aliases = [flags] + parts, [SM] + [ANY] * len(parts), {}
    if stack is not None:
        aliases = {len(args): 0}
        args += held(stack)
        specs.append(ANY)
    return pl.pallas_call(
        functools.partial(pack_kernel, places),
        out_shape=kept((GROUP, channels, channels), jnp.bfloat16),
        in_specs=specs,
        out_specs=ANY,
        scratch_shapes=[pltpu.SemaphoreType.DMA((len(parts),))],
        input_output_aliases=aliases,
        compiler_params=PARAMS,
        name="packed",
    )(*args)


def placed(stack, parts, member, row=0):
    for d, part in enumerate(parts):
        if part is not None:
            slot = jnp.bitwise_xor(member, d)
            stack = lax.dynamic_update_slice(stack, part[None], (slot, row, 0))
    return stack


def shifted(block, stage, to_stage):
    pairs = [(GROUP * stage + i, GROUP * to_stage + i) for i in range(MICROS)]
    return lax.ppermute(block, PIPE, pairs)


def traded(block, distance):
    pairs = [(i, i ^ distance) for i in range(lax.axis_size(PIPE)) if i % GROUP < MICROS]
    return lax.ppermute(block[distance], PIPE, pairs)


def together(block):
    return jnp.concatenate([block[0]] + [traded(block, d) for d in range(1, GROUP)])


def summed_part(block, axis):
    count = lax.axis_size(axis)
    parts = lax.all_to_all(block.reshape(count, -1, block.shape[1]), axis, 0, 0)
    return jnp.sum(parts.astype(jnp.float32), axis=0)


def all_parts(block, axis):
    count = lax.axis_size(axis)
    parts = lax.all_to_all(jnp.broadcast_to(block, (count,) + block.shape), axis, 0, 0)
    return parts.reshape(-1, block.shape[1])


def shards(base_ids, embed_table, segment_weights, conv_taps, norm_gains, cotangent):
    stages = lax.axis_size("g")
    member = lax.axis_index("q")
    flags = jnp.stack([lax.axis_index("g"), member]).astype(jnp.int32)
    micro = jnp.minimum(member, MICROS - 1)
    weight = segment_weights[0]
    channels = weight.shape[1]
    row_count = base_ids.shape[2]
    bf = jnp.bfloat16

    across = swapped(weight, 2)
    beside = swapped(weight, 1)
    own = jnp.concatenate([conv_taps[0], norm_gains, jnp.zeros((4, channels), jnp.float32)])
    own, base_ids, beside = lax.optimization_barrier((own, base_ids, beside))
    x = encode_bases(base_ids[0, micro], embed_table)
    par = placed(
        jnp.zeros((GROUP,) + own.shape, jnp.float32),
        [own] + [swapped(own, d) for d in range(1, GROUP)],
        member,
    )
    weights = packed(None, flags, [(0, 0, weight), (1, 0, beside)])
    across, weights, par, x = lax.optimization_barrier((across, weights, par, x))
    corner = swapped(across, 1)
    weights = packed(weights, flags, [(2, 0, across)])
    weights = packed(weights, flags, [(3, 0, corner)])

    wide = (GROUP, row_count, channels)
    h = jnp.zeros(wide, bf)
    e = jnp.zeros(wide, bf)
    states, k = [], None
    for stage in range(stages):
        skip, towers = stage == stages - 1, stage == 0
        outs = forward_stage(stage, skip, towers, flags, x, weights, par, k, h)
        states.append(outs[1:4])
        h = outs[4]
        if stage < stages - 1:
            x = shifted(outs[0], stage, stage + 1)
        if towers:
            x, tower = lax.optimization_barrier((x, outs[5]))
            k = shifted(tower, 0, stages - 1)

    g = cotangent[0, micro]
    returned = None
    for stage in reversed(range(stages)):
        last, first = stage == stages - 1, stage == 0
        outs = backward_stage(stage, last, first, flags, g, weights, par, states[stage], returned, e)
        e = outs[0]
        if stage > 0:
            g = shifted(outs[1], stage, stage - 1)
        if last:
            g, skip_grad = lax.optimization_barrier((g, outs[2]))
            returned = shifted(skip_grad, stages - 1, 0)
        if stage == stages - 2:
            h, e = lax.optimization_barrier((h, e))
            acts = together(h)
        if stage == 1:
            acts, e = lax.optimization_barrier((acts, e))
    errors = together(e)

    terms = lax.dot_general(acts, errors, (((0,), (0,)), ((), ())), preferred_element_type=jnp.float32)
    factor = 1.0 / math.sqrt(lax.axis_size(NEAR + ("yh",)) * MICROS * row_count)
    part = summed_part(terms.astype(bf), NEAR).astype(bf)
    part = (summed_part(part, "yh") * factor).astype(bf)
    whole = all_parts(all_parts(part, "yh"), NEAR)
    return whole.astype(jnp.float32)[None]


def solution(mesh):
    replicas, _ = mesh.devices.shape
    wide = math.gcd(4, replicas)
    low = math.gcd(2, replicas // wide)
    shape = (replicas // (wide * low), low, wide, -1, GROUP)
    grid = Mesh(mesh.devices.reshape(shape), ("yh", "yl", "x", "g", "q"))
    windows = P(("yh", "yl", "x"), None, None, None)
    return jax.shard_map(
        shards,
        mesh=grid,
        in_specs=(
            windows,
            P(),
            P(PIPE, None, None),
            P(PIPE, None, None),
            P(PIPE, None),
            windows,
        ),
        out_specs=P(PIPE, None, None),
        check_vma=False,
    )
```

```python
import functools
import math

import jax
import jax.numpy as jnp
from jax import lax
from jax.experimental import pallas as pl
from jax.experimental.pallas import tpu as pltpu
from jax.sharding import Mesh
from jax.sharding import PartitionSpec as P

GROUP = 4
MICROS = 3
CHUNK = 384
PIPE = ("g", "q")
NEAR = ("yl", "x")
ANY = pl.BlockSpec(memory_space=pl.ANY)
VM = pl.BlockSpec(memory_space=pltpu.VMEM)
SM = pl.BlockSpec(memory_space=pltpu.SMEM)
PARAMS = pltpu.CompilerParams(vmem_limit_bytes=6 * 1024 * 1024)
CUBIC = 0.044715
SCALE = math.sqrt(2.0 / math.pi)


def row_before(block):
    rows = lax.broadcasted_iota(jnp.int32, block.shape, 0)
    return jnp.where(rows == 0, 0.0, pltpu.roll(block, 1, 0))


def row_after(block):
    size = block.shape[0]
    rows = lax.broadcasted_iota(jnp.int32, block.shape, 0)
    return jnp.where(rows == size - 1, 0.0, pltpu.roll(block, size - 1, 0))


def chunks_of(channels):
    return [slice(c, c + CHUNK) for c in range(0, channels, CHUNK)]


def forward_kernel(stage, skip, towers, flags, x_ref, w_ref, par_ref, *rest):
    rest = list(rest)
    k_ref = rest.pop(0) if skip else None
    h_ref = rest.pop(0)
    y_ref, uh, gp, inv_b, hb = rest[:5]
    rest = rest[5:]
    ys = rest.pop(0) if towers else None
    (ub,) = rest
    channels = x_ref.shape[1]
    member = flags[1]
    active = (flags[0] == stage) & (member < MICROS)

    @pl.when(jnp.logical_not(active))
    def _():
        hb[...] = h_ref[...]

    @pl.when(active)
    def _():
        y = x_ref[...]
        for j in range(GROUP):
            d = jnp.bitwise_xor(member, j)
            squares = None
            for cs in chunks_of(channels):
                u = y[:, cs].astype(jnp.float32)
                if skip:
                    u = u + k_ref[j, :, cs].astype(jnp.float32)
                ub[:, cs] = u
                part = jnp.sum(u * u, axis=-1, keepdims=True)
                squares = part if squares is None else squares + part
            inv = lax.rsqrt(squares * (1.0 / channels) + 1e-06)
            inv_b[j] = jnp.broadcast_to(inv, inv_b.shape[1:])
            total = None
            for cs in chunks_of(channels):
                unit = ub[:, cs] * inv
                uh[j, :, cs] = unit
                n = unit * par_ref[j, 3:4, cs]
                v = (
                    par_ref[j, 0:1, cs] * row_before(n)
                    + par_ref[j, 1:2, cs] * n
                    + par_ref[j, 2:3, cs] * row_after(n)
                )
                v2 = v * v
                th = jnp.tanh(v * (SCALE + (SCALE * CUBIC) * v2))
                half = 0.5 * (1.0 + th)
                gp[j, :, cs] = half + (0.5 * v) * (1.0 - th * th) * (
                    SCALE + (3.0 * SCALE * CUBIC) * v2
                )
                act = (v * half).astype(jnp.bfloat16)
                hb[d, :, cs] = act
                part = jnp.dot(act, w_ref[j, cs, :], preferred_element_type=jnp.float32)
                total = part if total is None else total + part
            y = (ub[...] + total).astype(jnp.bfloat16)
            if towers:
                ys[j] = y
        y_ref[...] = y


def kept(shape, kind):
    return pltpu.VMEM(shape, kind)


def held(*arrays):
    return [pltpu.with_memory_space_constraint(a, pltpu.VMEM) for a in arrays]


def forward_stage(stage, skip, towers, flags, x, weights, par, k, h):
    rows, channels = x.shape
    f32, bf = jnp.float32, jnp.bfloat16
    wide = (GROUP, rows, channels)
    thin = (GROUP, rows, 128)
    out_shape = [
        kept((rows, channels), bf),
        kept(wide, f32),
        kept(wide, f32),
        kept(thin, f32),
        kept(wide, bf),
    ]
    if towers:
        out_shape.append(kept(wide, bf))
    args = [x, weights, par]
    if skip:
        args.append(k)
    args.append(h)
    args = [flags] + held(*args)
    return pl.pallas_call(
        functools.partial(forward_kernel, stage, skip, towers),
        out_shape=out_shape,
        in_specs=[SM] + [VM] * (len(args) - 1),
        out_specs=[VM] * len(out_shape),
        scratch_shapes=[pltpu.VMEM((rows, channels), f32)],
        input_output_aliases={len(args) - 1: 4},
        compiler_params=PARAMS,
        name=f"ahead{stage}",
    )(*args)


def backward_kernel(stage, last, first, flags, g_ref, w_ref, par_ref, uh, gp, inv_b, *rest):
    rest = list(rest)
    k_ref = rest.pop(0) if first else None
    e_ref = rest.pop(0)
    eb = rest.pop(0)
    dx_ref = None if first else rest.pop(0)
    gk_ref = rest.pop(0) if last else None
    gb, mb = rest
    channels = g_ref.shape[1]
    member = flags[1]
    active = (flags[0] == stage) & (member < MICROS)

    @pl.when(jnp.logical_not(active))
    def _():
        eb[...] = e_ref[...]

    @pl.when(active)
    def _():
        dx = g_ref[...]
        for j in reversed(range(GROUP)):
            d = jnp.bitwise_xor(member, j)
            for cs in chunks_of(channels):
                g = dx[:, cs].astype(jnp.float32)
                if first:
                    g = g + k_ref[j, :, cs].astype(jnp.float32)
                gb[:, cs] = g
            e = gb[...].astype(jnp.bfloat16)
            eb[d] = e
            if first and j == 0:
                continue
            dots = None
            for cs in chunks_of(channels):
                da = lax.dot_general(
                    e, w_ref[j, cs, :], (((1,), (1,)), ((), ())), preferred_element_type=jnp.float32
                )
                dv = da * gp[j, :, cs]
                dn = (
                    par_ref[j, 0:1, cs] * row_after(dv)
                    + par_ref[j, 1:2, cs] * dv
                    + par_ref[j, 2:3, cs] * row_before(dv)
                )
                m = dn * par_ref[j, 3:4, cs]
                mb[:, cs] = m
                part = jnp.sum(m * uh[j, :, cs], axis=-1, keepdims=True)
                dots = part if dots is None else dots + part
            mean = dots * (1.0 / channels)
            inv = inv_b[j, :, 0:1]
            dx = (gb[...] + inv * (mb[...] - uh[j] * mean)).astype(jnp.bfloat16)
            if last:
                gk_ref[j] = dx
        if not first:
            dx_ref[...] = dx


def backward_stage(stage, last, first, flags, g, weights, par, state, k, e):
    rows, channels = g.shape
    f32, bf = jnp.float32, jnp.bfloat16
    wide = (GROUP, rows, channels)
    args = [g, weights, par, *state]
    if first:
        args.append(k)
    args.append(e)
    args = [flags] + held(*args)
    out_shape = [kept(wide, bf)]
    if not first:
        out_shape.append(kept((rows, channels), bf))
    if last:
        out_shape.append(kept(wide, bf))
    return pl.pallas_call(
        functools.partial(backward_kernel, stage, last, first),
        out_shape=out_shape,
        in_specs=[SM] + [VM] * (len(args) - 1),
        out_specs=[VM] * len(out_shape),
        scratch_shapes=[pltpu.VMEM((rows, channels), f32)] * 2,
        input_output_aliases={len(args) - 1: 0},
        compiler_params=PARAMS,
        name=f"behind{stage}",
    )(*args)


def turn_kernel(stage, flags, x_ref, w_ref, par_ref, k_ref, g_ref, h_ref, e_ref, *rest):
    h_out, e_out, dx_ref, gk_ref, y, uh, gp, inv_b, ub, gb, mb = rest
    forward_kernel(stage, True, False, flags, x_ref, w_ref, par_ref, k_ref, h_ref, y, uh, gp, inv_b, h_out, ub)
    backward_kernel(stage, True, False, flags, g_ref, w_ref, par_ref, uh, gp, inv_b, e_ref, e_out, dx_ref, gk_ref, gb, mb)


def turning_stage(stage, flags, x, weights, par, k, g, h, e):
    rows, channels = x.shape
    f32, bf = jnp.float32, jnp.bfloat16
    wide = (GROUP, rows, channels)
    args = [flags] + held(x, weights, par, k, g, h, e)
    full = pltpu.VMEM((rows, channels), f32)
    return pl.pallas_call(
        functools.partial(turn_kernel, stage),
        out_shape=[kept(wide, bf), kept(wide, bf), kept((rows, channels), bf), kept(wide, bf)],
        in_specs=[SM] + [VM] * (len(args) - 1),
        out_specs=[VM] * 4,
        scratch_shapes=[
            pltpu.VMEM((rows, channels), bf),
            pltpu.VMEM(wide, f32),
            pltpu.VMEM(wide, f32),
            pltpu.VMEM((GROUP, rows, 128), f32),
            full,
            full,
            full,
        ],
        input_output_aliases={6: 0, 7: 1},
        compiler_params=PARAMS,
        name=f"turn{stage}",
    )(*args)


def encode_bases(base_rows, embed_table):
    one_hot = (base_rows[:, :, None] == jnp.arange(4, dtype=jnp.int32)).astype(jnp.bfloat16)
    one_hot = one_hot.reshape(base_rows.shape[0], -1)
    return jnp.dot(one_hot, embed_table, preferred_element_type=jnp.float32).astype(jnp.bfloat16)


def swapped(block, distance):
    pairs = [(i, i ^ distance) for i in range(lax.axis_size(PIPE))]
    return lax.ppermute(block, PIPE, pairs)


def pack_kernel(places, flags, *rest):
    parts, out, sems = rest[: len(places)], rest[-2], rest[-1]
    copies = []
    for i, ((d, row), part) in enumerate(zip(places, parts)):
        slot = jnp.bitwise_xor(flags[1], d)
        target = out.at[slot, pl.ds(row, part.shape[0]), :]
        copies.append(pltpu.make_async_copy(part, target, sems.at[i]))
        copies[-1].start()
    for copy in copies:
        copy.wait()


def packed(stack, flags, items):
    places = [(d, row) for d, row, _ in items]
    parts = [part for _, _, part in items]
    channels = parts[0].shape[1]
    args, specs, aliases = [flags] + parts, [SM] + [ANY] * len(parts), {}
    if stack is not None:
        aliases = {len(args): 0}
        args += held(stack)
        specs.append(ANY)
    return pl.pallas_call(
        functools.partial(pack_kernel, places),
        out_shape=kept((GROUP, channels, channels), jnp.bfloat16),
        in_specs=specs,
        out_specs=ANY,
        scratch_shapes=[pltpu.SemaphoreType.DMA((len(parts),))],
        input_output_aliases=aliases,
        compiler_params=PARAMS,
        name="packed",
    )(*args)


def placed(stack, parts, member, row=0):
    for d, part in enumerate(parts):
        if part is not None:
            slot = jnp.bitwise_xor(member, d)
            stack = lax.dynamic_update_slice(stack, part[None], (slot, row, 0))
    return stack


def shifted(block, stage, to_stage):
    pairs = [(GROUP * stage + i, GROUP * to_stage + i) for i in range(MICROS)]
    return lax.ppermute(block, PIPE, pairs)


def traded(block, distance):
    pairs = [(i, i ^ distance) for i in range(lax.axis_size(PIPE)) if i % GROUP < MICROS]
    return lax.ppermute(block[distance], PIPE, pairs)


def together(block):
    return jnp.concatenate([block[0]] + [traded(block, d) for d in range(1, GROUP)])


def summed_part(block, axis):
    count = lax.axis_size(axis)
    parts = lax.all_to_all(block.reshape(count, -1, block.shape[1]), axis, 0, 0)
    return jnp.sum(parts.astype(jnp.float32), axis=0)


def all_parts(block, axis):
    count = lax.axis_size(axis)
    parts = lax.all_to_all(jnp.broadcast_to(block, (count,) + block.shape), axis, 0, 0)
    return parts.reshape(-1, block.shape[1])


def shards(base_ids, embed_table, segment_weights, conv_taps, norm_gains, cotangent):
    stages = lax.axis_size("g")
    member = lax.axis_index("q")
    flags = jnp.stack([lax.axis_index("g"), member]).astype(jnp.int32)
    micro = jnp.minimum(member, MICROS - 1)
    weight = segment_weights[0]
    channels = weight.shape[1]
    row_count = base_ids.shape[2]
    bf = jnp.bfloat16

    across = swapped(weight, 2)
    beside = swapped(weight, 1)
    own = jnp.concatenate([conv_taps[0], norm_gains, jnp.zeros((4, channels), jnp.float32)])
    own, base_ids, beside = lax.optimization_barrier((own, base_ids, beside))
    x = encode_bases(base_ids[0, micro], embed_table)
    par = placed(
        jnp.zeros((GROUP,) + own.shape, jnp.float32),
        [own] + [swapped(own, d) for d in range(1, GROUP)],
        member,
    )
    weights = packed(None, flags, [(0, 0, weight), (1, 0, beside)])
    across, weights, par, x = lax.optimization_barrier((across, weights, par, x))
    corner = swapped(across, 1)
    weights = packed(weights, flags, [(2, 0, across)])
    weights = packed(weights, flags, [(3, 0, corner)])

    wide = (GROUP, row_count, channels)
    h = jnp.zeros(wide, bf)
    e = jnp.zeros(wide, bf)
    states, k = [], None
    for stage in range(stages - 1):
        towers = stage == 0
        outs = forward_stage(stage, False, towers, flags, x, weights, par, k, h)
        states.append(outs[1:4])
        h = outs[4]
        x = shifted(outs[0], stage, stage + 1)
        if towers:
            x, tower = lax.optimization_barrier((x, outs[5]))
            k = shifted(tower, 0, stages - 1)

    h, e, dx, skip_grad = turning_stage(stages - 1, flags, x, weights, par, k, cotangent[0, micro], h, e)
    g = shifted(dx, stages - 1, stages - 2)
    g, skip_grad = lax.optimization_barrier((g, skip_grad))
    returned = shifted(skip_grad, stages - 1, 0)
    for stage in reversed(range(stages - 1)):
        first = stage == 0
        outs = backward_stage(stage, False, first, flags, g, weights, par, states[stage], returned, e)
        e = outs[0]
        if stage > 0:
            g = shifted(outs[1], stage, stage - 1)
        if stage == stages - 2:
            h, e = lax.optimization_barrier((h, e))
            acts = together(h)
        if stage == 1:
            acts, e = lax.optimization_barrier((acts, e))
    errors = together(e)

    terms = lax.dot_general(acts, errors, (((0,), (0,)), ((), ())), preferred_element_type=jnp.float32)
    factor = 1.0 / math.sqrt(lax.axis_size(NEAR + ("yh",)) * MICROS * row_count)
    part = summed_part(terms.astype(bf), NEAR).astype(bf)
    part = (summed_part(part, "yh") * factor).astype(bf)
    whole = all_parts(all_parts(part, "yh"), NEAR)
    return whole.astype(jnp.float32)[None]


def solution(mesh):
    replicas, _ = mesh.devices.shape
    wide = math.gcd(4, replicas)
    low = math.gcd(2, replicas // wide)
    shape = (replicas // (wide * low), low, wide, -1, GROUP)
    grid = Mesh(mesh.devices.reshape(shape), ("yh", "yl", "x", "g", "q"))
    windows = P(("yh", "yl", "x"), None, None, None)
    return jax.shard_map(
        shards,
        mesh=grid,
        in_specs=(
            windows,
            P(),
            P(PIPE, None, None),
            P(PIPE, None, None),
            P(PIPE, None),
            windows,
        ),
        out_specs=P(PIPE, None, None),
        check_vma=False,
    )
```

```python
import functools
import math

import jax
import jax.numpy as jnp
from jax import lax
from jax.experimental import pallas as pl
from jax.experimental.pallas import tpu as pltpu
from jax.sharding import Mesh
from jax.sharding import PartitionSpec as P

GROUP = 4
MICROS = 3
CHUNK = 384
PIPE = ("g", "q")
NEAR = ("yl", "x")
ANY = pl.BlockSpec(memory_space=pl.ANY)
VM = pl.BlockSpec(memory_space=pltpu.VMEM)
SM = pl.BlockSpec(memory_space=pltpu.SMEM)
PARAMS = pltpu.CompilerParams(vmem_limit_bytes=4 * 1024 * 1024)
CUBIC = 0.044715
SCALE = math.sqrt(2.0 / math.pi)


def row_before(block):
    rows = lax.broadcasted_iota(jnp.int32, block.shape, 0)
    return jnp.where(rows == 0, 0.0, pltpu.roll(block, 1, 0))


def row_after(block):
    size = block.shape[0]
    rows = lax.broadcasted_iota(jnp.int32, block.shape, 0)
    return jnp.where(rows == size - 1, 0.0, pltpu.roll(block, size - 1, 0))


def chunks_of(channels):
    return [slice(c, c + CHUNK) for c in range(0, channels, CHUNK)]


def forward_kernel(stage, skip, towers, flags, x_ref, w_ref, par_ref, *rest):
    rest = list(rest)
    k_ref = rest.pop(0) if skip else None
    h_ref = rest.pop(0)
    y_ref, uh, gp, inv_b, hb = rest[:5]
    rest = rest[5:]
    ys = rest.pop(0) if towers else None
    (ub,) = rest
    channels = x_ref.shape[1]
    member = flags[1]
    active = (flags[0] == stage) & (member < MICROS)

    @pl.when(jnp.logical_not(active))
    def _():
        hb[...] = h_ref[...]

    @pl.when(active)
    def _():
        y = x_ref[...]
        for j in range(GROUP):
            d = jnp.bitwise_xor(member, j)
            squares = None
            for cs in chunks_of(channels):
                u = y[:, cs].astype(jnp.float32)
                if skip:
                    u = u + k_ref[j, :, cs].astype(jnp.float32)
                ub[:, cs] = u
                part = jnp.sum(u * u, axis=-1, keepdims=True)
                squares = part if squares is None else squares + part
            inv = lax.rsqrt(squares * (1.0 / channels) + 1e-06)
            inv_b[j] = jnp.broadcast_to(inv, inv_b.shape[1:])
            total = None
            for cs in chunks_of(channels):
                unit = ub[:, cs] * inv
                uh[j, :, cs] = unit
                n = unit * par_ref[j, 3:4, cs]
                v = (
                    par_ref[j, 0:1, cs] * row_before(n)
                    + par_ref[j, 1:2, cs] * n
                    + par_ref[j, 2:3, cs] * row_after(n)
                )
                v2 = v * v
                th = jnp.tanh(v * (SCALE + (SCALE * CUBIC) * v2))
                half = 0.5 * (1.0 + th)
                gp[j, :, cs] = half + (0.5 * v) * (1.0 - th * th) * (
                    SCALE + (3.0 * SCALE * CUBIC) * v2
                )
                act = (v * half).astype(jnp.bfloat16)
                hb[d, :, cs] = act
                part = jnp.dot(act, w_ref[j, cs, :], preferred_element_type=jnp.float32)
                total = part if total is None else total + part
            y = (ub[...] + total).astype(jnp.bfloat16)
            if towers:
                ys[j] = y
        y_ref[...] = y


def kept(shape, kind):
    return pltpu.VMEM(shape, kind)


def held(*arrays):
    return [pltpu.with_memory_space_constraint(a, pltpu.VMEM) for a in arrays]


def forward_stage(stage, skip, towers, flags, x, weights, par, k, h):
    rows, channels = x.shape
    f32, bf = jnp.float32, jnp.bfloat16
    wide = (GROUP, rows, channels)
    thin = (GROUP, rows, 128)
    out_shape = [
        kept((rows, channels), bf),
        kept(wide, f32),
        kept(wide, f32),
        kept(thin, f32),
        kept(wide, bf),
    ]
    if towers:
        out_shape.append(kept(wide, bf))
    args = [x, weights, par]
    if skip:
        args.append(k)
    args.append(h)
    args = [flags] + held(*args)
    return pl.pallas_call(
        functools.partial(forward_kernel, stage, skip, towers),
        out_shape=out_shape,
        in_specs=[SM] + [VM] * (len(args) - 1),
        out_specs=[VM] * len(out_shape),
        scratch_shapes=[pltpu.VMEM((rows, channels), f32)],
        input_output_aliases={len(args) - 1: 4},
        compiler_params=PARAMS,
        name=f"ahead{stage}",
    )(*args)


def backward_kernel(stage, last, first, flags, g_ref, w_ref, par_ref, uh, gp, inv_b, *rest):
    rest = list(rest)
    k_ref = rest.pop(0) if first else None
    e_ref = rest.pop(0)
    eb = rest.pop(0)
    dx_ref = None if first else rest.pop(0)
    gk_ref = rest.pop(0) if last else None
    gb, mb = rest
    channels = g_ref.shape[1]
    member = flags[1]
    active = (flags[0] == stage) & (member < MICROS)

    @pl.when(jnp.logical_not(active))
    def _():
        eb[...] = e_ref[...]

    @pl.when(active)
    def _():
        dx = g_ref[...]
        for j in reversed(range(GROUP)):
            d = jnp.bitwise_xor(member, j)
            if first:
                gb[...] = dx.astype(jnp.float32) + k_ref[j].astype(jnp.float32)
                e = gb[...].astype(jnp.bfloat16)
            else:
                gb[...] = dx.astype(jnp.float32)
                e = dx
            eb[d] = e
            if first and j == 0:
                continue
            dots = None
            for cs in chunks_of(channels):
                da = lax.dot_general(
                    e, w_ref[j, cs, :], (((1,), (1,)), ((), ())), preferred_element_type=jnp.float32
                )
                dv = da * gp[j, :, cs]
                dn = (
                    par_ref[j, 0:1, cs] * row_after(dv)
                    + par_ref[j, 1:2, cs] * dv
                    + par_ref[j, 2:3, cs] * row_before(dv)
                )
                m = dn * par_ref[j, 3:4, cs]
                mb[:, cs] = m
                part = jnp.sum(m * uh[j, :, cs], axis=-1, keepdims=True)
                dots = part if dots is None else dots + part
            mean = dots * (1.0 / channels)
            inv = inv_b[j, :, 0:1]
            dx = (gb[...] + inv * (mb[...] - uh[j] * mean)).astype(jnp.bfloat16)
            if last:
                gk_ref[j] = dx
        if not first:
            dx_ref[...] = dx


def backward_stage(stage, last, first, flags, g, weights, par, state, k, e):
    rows, channels = g.shape
    f32, bf = jnp.float32, jnp.bfloat16
    wide = (GROUP, rows, channels)
    args = [g, weights, par, *state]
    if first:
        args.append(k)
    args.append(e)
    args = [flags] + held(*args)
    out_shape = [kept(wide, bf)]
    if not first:
        out_shape.append(kept((rows, channels), bf))
    if last:
        out_shape.append(kept(wide, bf))
    return pl.pallas_call(
        functools.partial(backward_kernel, stage, last, first),
        out_shape=out_shape,
        in_specs=[SM] + [VM] * (len(args) - 1),
        out_specs=[VM] * len(out_shape),
        scratch_shapes=[pltpu.VMEM((rows, channels), f32)] * 2,
        input_output_aliases={len(args) - 1: 0},
        compiler_params=PARAMS,
        name=f"behind{stage}",
    )(*args)


def encode_bases(base_rows, embed_table):
    one_hot = (base_rows[:, :, None] == jnp.arange(4, dtype=jnp.int32)).astype(jnp.bfloat16)
    one_hot = one_hot.reshape(base_rows.shape[0], -1)
    return jnp.dot(one_hot, embed_table, preferred_element_type=jnp.float32).astype(jnp.bfloat16)


def swapped(block, distance):
    pairs = [(i, i ^ distance) for i in range(lax.axis_size(PIPE))]
    return lax.ppermute(block, PIPE, pairs)


def pack_kernel(places, flags, *rest):
    parts, out, sems = rest[: len(places)], rest[-2], rest[-1]
    copies = []
    for i, ((d, row), part) in enumerate(zip(places, parts)):
        slot = jnp.bitwise_xor(flags[1], d)
        target = out.at[slot, pl.ds(row, part.shape[0]), :]
        copies.append(pltpu.make_async_copy(part, target, sems.at[i]))
        copies[-1].start()
    for copy in copies:
        copy.wait()


def packed(stack, flags, items):
    places = [(d, row) for d, row, _ in items]
    parts = [part for _, _, part in items]
    channels = parts[0].shape[1]
    args, specs, aliases = [flags] + parts, [SM] + [ANY] * len(parts), {}
    if stack is not None:
        aliases = {len(args): 0}
        args += held(stack)
        specs.append(ANY)
    return pl.pallas_call(
        functools.partial(pack_kernel, places),
        out_shape=kept((GROUP, channels, channels), jnp.bfloat16),
        in_specs=specs,
        out_specs=ANY,
        scratch_shapes=[pltpu.SemaphoreType.DMA((len(parts),))],
        input_output_aliases=aliases,
        compiler_params=PARAMS,
        name="packed",
    )(*args)


def placed(stack, parts, member, row=0):
    for d, part in enumerate(parts):
        if part is not None:
            slot = jnp.bitwise_xor(member, d)
            stack = lax.dynamic_update_slice(stack, part[None], (slot, row, 0))
    return stack


def shifted(block, stage, to_stage):
    pairs = [(GROUP * stage + i, GROUP * to_stage + i) for i in range(MICROS)]
    return lax.ppermute(block, PIPE, pairs)


def traded(block, distance):
    pairs = [(i, i ^ distance) for i in range(lax.axis_size(PIPE)) if i % GROUP < MICROS]
    return lax.ppermute(block[distance], PIPE, pairs)


def together(block):
    return jnp.concatenate([block[0]] + [traded(block, d) for d in range(1, GROUP)])


def summed_part(block, axis):
    count = lax.axis_size(axis)
    parts = lax.all_to_all(block.reshape(count, -1, block.shape[1]), axis, 0, 0)
    return jnp.sum(parts.astype(jnp.float32), axis=0)


def all_parts(block, axis):
    count = lax.axis_size(axis)
    parts = lax.all_to_all(jnp.broadcast_to(block, (count,) + block.shape), axis, 0, 0)
    return parts.reshape(-1, block.shape[1])


def shards(base_ids, embed_table, segment_weights, conv_taps, norm_gains, cotangent):
    stages = lax.axis_size("g")
    member = lax.axis_index("q")
    flags = jnp.stack([lax.axis_index("g"), member]).astype(jnp.int32)
    micro = jnp.minimum(member, MICROS - 1)
    weight = segment_weights[0]
    channels = weight.shape[1]
    row_count = base_ids.shape[2]
    bf = jnp.bfloat16

    across = swapped(weight, 2)
    beside = swapped(weight, 1)
    own = jnp.concatenate([conv_taps[0], norm_gains, jnp.zeros((4, channels), jnp.float32)])
    own, base_ids, beside = lax.optimization_barrier((own, base_ids, beside))
    x = encode_bases(base_ids[0, micro], embed_table)
    par = placed(
        jnp.zeros((GROUP,) + own.shape, jnp.float32),
        [own] + [swapped(own, d) for d in range(1, GROUP)],
        member,
    )
    weights = packed(None, flags, [(0, 0, weight), (1, 0, beside)])
    across, weights, par, x = lax.optimization_barrier((across, weights, par, x))
    corner = swapped(across, 1)
    weights = packed(weights, flags, [(2, 0, across)])
    weights = packed(weights, flags, [(3, 0, corner)])

    wide = (GROUP, row_count, channels)
    h = jnp.zeros(wide, bf)
    e = jnp.zeros(wide, bf)
    states, k = [], None
    for stage in range(stages):
        skip, towers = stage == stages - 1, stage == 0
        outs = forward_stage(stage, skip, towers, flags, x, weights, par, k, h)
        states.append(outs[1:4])
        h = outs[4]
        if stage < stages - 1:
            x = shifted(outs[0], stage, stage + 1)
        if towers:
            x, tower = lax.optimization_barrier((x, outs[5]))
            k = shifted(tower, 0, stages - 1)

    g = cotangent[0, micro]
    returned = None
    for stage in reversed(range(stages)):
        last, first = stage == stages - 1, stage == 0
        outs = backward_stage(stage, last, first, flags, g, weights, par, states[stage], returned, e)
        e = outs[0]
        if stage > 0:
            g = shifted(outs[1], stage, stage - 1)
        if last:
            g, skip_grad = lax.optimization_barrier((g, outs[2]))
            returned = shifted(skip_grad, stages - 1, 0)
        if stage == stages - 2:
            h, e = lax.optimization_barrier((h, e))
            acts = together(h)
        if stage == 1:
            acts, e = lax.optimization_barrier((acts, e))
    errors = together(e)

    terms = lax.dot_general(acts, errors, (((0,), (0,)), ((), ())), preferred_element_type=jnp.float32)
    factor = 1.0 / math.sqrt(lax.axis_size(NEAR + ("yh",)) * MICROS * row_count)
    part = summed_part(terms.astype(bf), NEAR).astype(bf)
    part = (summed_part(part, "yh") * factor).astype(bf)
    whole = all_parts(all_parts(part, "yh"), NEAR)
    return whole.astype(jnp.float32)[None]


def solution(mesh):
    replicas, _ = mesh.devices.shape
    wide = math.gcd(4, replicas)
    low = math.gcd(2, replicas // wide)
    shape = (replicas // (wide * low), low, wide, -1, GROUP)
    grid = Mesh(mesh.devices.reshape(shape), ("yh", "yl", "x", "g", "q"))
    windows = P(("yh", "yl", "x"), None, None, None)
    return jax.shard_map(
        shards,
        mesh=grid,
        in_specs=(
            windows,
            P(),
            P(PIPE, None, None),
            P(PIPE, None, None),
            P(PIPE, None),
            windows,
        ),
        out_specs=P(PIPE, None, None),
        check_vma=False,
    )
```
